32 devices in a mesh: ctx: 8 (over z, x), tp: 4 (over y, core).
Axes of the slice: x: 2, y: 2, z: 4, core: 2. Of those that a mesh axis runs over, the one named last changes fastest.
Arguments:
- queries: bfloat16 [2048, 8192], P('ctx', 'tp'), may hold values from -6 to 6
- key_proj: bfloat16 [2048, 8192], P('ctx', 'tp'), may hold values from -6 to 6
- values: bfloat16 [2048, 8192], P('ctx', 'tp'), may hold values from -6 to 6
- residues: float32 [16, 8192], P(None, 'tp'), may hold values from -0.4 to 0.4
- decay_rates: float32 [16, 8192], P(None, 'tp'), may hold values from 0 to 0.034, as said below
- skip_weight: float32 [8192], P('tp'), may hold values from 0.5 to 1.5
- stream: bfloat16 [2048, 8192], P('ctx', 'tp'), may hold values from -110 to 110
- norm_gain: float32 [8192], P('tp'), may hold values from 0.1 to 1.9
Outputs:
- new_stream: bfloat16 [2048, 8192], P('ctx', 'tp')
- normed: bfloat16 [2048, 8192], P('ctx', 'tp')
The draws below stay inside these ranges and needn't reach their ends.
Inputs may be any that keep to these rules, and one draw needn't show every extreme that they name: `decay_rates`: each mode's decay per position; all positive.
All inputs are finite; a program needn't handle non-finite values.
Results may differ from the reference program's by a relative error of at most 0.007.
Values may be sent and summed in bfloat16 or wider, within the bound.
A program may use at most 128 MiB of HBM per device.

```python
import math
import jax
import jax.numpy as jnp
from jax import lax

D = 8192
MODES = 16
SEQ = 2048


def modal_rates(key, lowest, highest):
    fraction = jax.random.uniform(key, (MODES, D), jnp.float32)
    return jnp.exp(jnp.log(lowest) + fraction * (jnp.log(highest) - jnp.log(lowest)))


def draw_decay_rates(key, part):
    return modal_rates(key, 0.5 / SEQ, 1.0 / 30.0)


def draw_residues(key, part):
    decay = modal_rates(key, 0.5 / SEQ, 1.0 / 30.0)
    key = jax.random.fold_in(key, 7)
    base = 0.25 * jnp.clip(jax.random.normal(key, (MODES, D), jnp.float32), -6.0, 6.0)
    return base * jnp.sqrt(2.0 * decay)


def draw_stream(key, part):
    key = jax.random.fold_in(key, 5)
    key_cols, key_rows, key_base = jax.random.split(key, 3)
    ramp = jnp.arange(D, dtype=jnp.float32) / D
    spread = 10.0 ** jax.random.uniform(key_cols, (D,), jnp.float32)
    row_scale = 10.0 ** jax.random.uniform(key_rows, (SEQ, 1), jnp.float32, -0.5, 0.5)
    column_scale = 3.0 ** ramp * spread / 6.0
    base = jnp.clip(jax.random.normal(key_base, (SEQ, D), jnp.float32), -6.0, 6.0)
    return (base * row_scale * column_scale[None, :]).astype(jnp.bfloat16)


def steps_of(rng, shape, cuts, least, largest):
    def one(position, parts):
        draws = jax.random.uniform(jax.random.fold_in(jax.random.fold_in(rng, 6), position), (parts,), jnp.float32, least / len(cuts), largest / len(cuts))
        return jnp.repeat(jnp.exp(draws), shape[position] // parts).reshape((-1,) + (1,) * (len(shape) - position - 1))

    gain = one(*cuts[0])
    for cut in cuts[1:]:
        gain = gain * one(*cut)
    return gain


def centred(rng, extent, scale, most, cuts=(), held_as=jnp.bfloat16):
    values = scale * jax.random.normal(rng, extent, jnp.float32)
    if cuts:
        values = values * steps_of(rng, extent, cuts, -0.22, 0.18)
    return jnp.clip(values, -most, most).astype(held_as)


def setup_inputs(seed: int = 0) -> dict:
    splits = jax.random.split(jax.random.key(seed), 9)
    return {
        "queries": centred(splits[0], (SEQ, D), 1.0, 6.0, ((0, 8), (1, 4))),
        "key_proj": centred(splits[1], (SEQ, D), 1.0, 6.0, ((0, 8), (1, 4))),
        "values": centred(splits[2], (SEQ, D), 1.0, 6.0, ((0, 8), (1, 4))),
        "residues": draw_residues(jax.random.fold_in(splits[8], 71), 0),
        "decay_rates": draw_decay_rates(jax.random.fold_in(splits[8], 71), 0),
        "skip_weight": jnp.clip(0.5 + 1.0 * jax.random.uniform(splits[5], (D,), jnp.float32) ** steps_of(splits[5], (D,), ((0, 4),), -0.2, 0.2), 0.5, 1.5),
        "stream": draw_stream(jax.random.fold_in(splits[8], 71), 0),
        "norm_gain": jnp.clip(1.0 + 0.18 * jax.random.normal(splits[7], (D,), jnp.float32), 0.1, 1.9),
    }


epsilon = 1e-06

def reference(queries, key_proj, values, residues, decay_rates, skip_weight, stream, norm_gain):
    signal = (queries.astype(jnp.float32) * key_proj.astype(jnp.float32)).astype(jnp.bfloat16)
    widened = lax.optimization_barrier(signal).astype(jnp.float32)
    channel_group = math.gcd(D, 256)
    group_count = D // channel_group

    def split_groups(source, length):
        return source.reshape(length, group_count, channel_group).transpose(1, 0, 2)

    def conv_group(pieces):
        part_signal, part_decay, part_residue = pieces
        positions = jnp.arange(SEQ, dtype=jnp.float32)[:, None]
        kernel_taps = jnp.zeros((SEQ, channel_group), jnp.float32)
        for mode_index in range(MODES):
            kernel_taps = kernel_taps + part_residue[mode_index] * jnp.exp(-part_decay[mode_index] * positions)
        spectrum = jnp.fft.rfft(part_signal, n=2 * SEQ, axis=0) * jnp.fft.rfft(kernel_taps, n=2 * SEQ, axis=0)
        return jnp.fft.irfft(spectrum, n=2 * SEQ, axis=0)[:SEQ]
    convolved = lax.map(conv_group, (split_groups(widened, SEQ), split_groups(decay_rates, MODES), split_groups(residues, MODES)))
    convolved = convolved.transpose(1, 0, 2).reshape(SEQ, D)
    mixed = values.astype(jnp.float32) * (convolved + skip_weight[None, :] * widened)
    new_stream = (stream.astype(jnp.float32) + mixed).astype(jnp.bfloat16)
    restored = lax.optimization_barrier(new_stream).astype(jnp.float32)
    row_power = lax.optimization_barrier(jnp.mean(restored * restored, axis=1, keepdims=True))
    normed = (restored * lax.rsqrt(row_power + epsilon) * norm_gain[None, :]).astype(jnp.bfloat16)
    return (new_stream, normed)
```

```python
import functools
import math

import jax
import jax.numpy as jnp
import numpy as np
from jax import lax
from jax.experimental import pallas as pl
from jax.experimental.pallas import tpu as pltpu
from jax.sharding import PartitionSpec as P

epsilon = 1e-06
lane = 128
sub = 8
dft_cols = 256
MESH = pl.DeviceIdType.MESH
f32 = jnp.float32
bf16 = jnp.bfloat16


def dft_tables(rows):
    freq = np.arange(rows)[:, None]
    pos = np.arange(rows)[None, :]
    angle = math.pi * (((2 * freq + 1) * pos) % (4 * rows)) / (2 * rows)
    forward = np.concatenate([np.cos(angle), -np.sin(angle)], axis=0)
    inverse = np.concatenate([np.cos(angle).T, -np.sin(angle).T], axis=1) / rows
    return forward.astype(bf16), inverse.astype(bf16)


def body(
    n_ctx, n_tp, n_sub, per_dev,
    q_hbm, k_hbm, v_hbm, res_hbm, dec_hbm, skip_hbm, str_hbm, gain_hbm, fwd_hbm, inv_hbm,
    new_hbm, norm_hbm,
    q, k, v, res, dec, skip, stream, gain, fwd, inv,
    sig, taps, conv, new, norm, ends, decay_pow, got, starts, states, square, row_sums,
    in_sem, out_sem, send1, recv1, send2, recv2, send3, recv3,
):
    rows, width = q.shape
    modes = res.shape[0]
    n_lane = width // lane
    part = modes // n_sub
    me = lax.axis_index("ctx")
    tp = lax.axis_index("tp")

    loads = {}
    order = [
        ("dec", dec_hbm, dec), ("q", q_hbm, q), ("k", k_hbm, k), ("res", res_hbm, res),
        ("fwd", fwd_hbm, fwd), ("inv", inv_hbm, inv), ("v", v_hbm, v),
        ("stream", str_hbm, stream), ("skip", skip_hbm, skip), ("gain", gain_hbm, gain),
    ]
    for i, (name, src, dst) in enumerate(order):
        loads[name] = pltpu.make_async_copy(src, dst, in_sem.at[i])
        loads[name].start()

    barrier = pltpu.get_barrier_semaphore()
    for d in range(1, n_ctx):
        pl.semaphore_signal(barrier, inc=1, device_id={"ctx": lax.rem(me + d, n_ctx)}, device_id_type=MESH)
    for d in range(1, n_tp):
        pl.semaphore_signal(barrier, inc=1, device_id={"tp": lax.rem(tp + d, n_tp)}, device_id_type=MESH)

    sublane = lax.broadcasted_iota(jnp.int32, (sub, lane), 0).astype(f32)

    def lanes_of(t):
        return pl.ds(pl.multiple_of(t * lane, lane), lane)

    def spread(x, n):
        return jnp.broadcast_to(x[n:n + 1, :], (sub, lane))

    for name in ("dec", "q", "k"):
        loads[name].wait()

    def end_states(t, _):
        cols = lanes_of(t)
        rate = dec[:, cols]
        step = jnp.exp(rate * (-float(sub)))
        steps = [spread(step, n) for n in range(modes)]

        def block(m, acc):
            at = pl.ds(pl.multiple_of(m * 16, 16), 16)
            s = (q[at, cols].astype(f32) * k[at, cols].astype(f32)).astype(bf16)
            sig[at, cols] = s
            s = s.astype(f32)
            acc = tuple(a * b + s[:8] for a, b in zip(acc, steps))
            return tuple(a * b + s[8:] for a, b in zip(acc, steps))

        acc = lax.fori_loop(0, rows // 16, block, (jnp.zeros((sub, lane), f32),) * modes, unroll=4)
        total = jnp.concatenate(
            [
                jnp.sum(a * jnp.exp(-spread(rate, n) * (sub - 1.0 - sublane)), axis=0, keepdims=True)
                for n, a in enumerate(acc)
            ],
            axis=0,
        )
        power = jnp.exp(rate * (-float(rows)))
        for g in range(n_sub):
            ends[t * n_sub + g] = total[g * part:(g + 1) * part]
            decay_pow[t * n_sub + g] = power[g * part:(g + 1) * part]
        return 0

    lax.fori_loop(0, n_lane, end_states, 0)

    pl.semaphore_wait(barrier, n_ctx - 1 + n_tp - 1)

    mine = pl.ds(me * per_dev, per_dev)
    first = []
    for d in range(1, n_ctx):
        to = lax.rem(me + d, n_ctx)
        copy = pltpu.make_async_remote_copy(
            src_ref=ends.at[pl.ds(to * per_dev, per_dev)], dst_ref=got.at[me],
            send_sem=send1.at[d], recv_sem=recv1.at[d], device_id={"ctx": to}, device_id_type=MESH,
        )
        copy.start()
        first.append(copy)

    def modal(coefs, steps, emit):
        def block(m, z):
            top = sum(z[1:], z[0])
            z = tuple(a * b for a, b in zip(z, steps))
            low = sum(z[1:], z[0])
            z = tuple(a * b for a, b in zip(z, steps))
            emit(pl.ds(pl.multiple_of(m * 16, 16), 16), jnp.concatenate([top, low], axis=0))
            return z

        lax.fori_loop(0, rows // 16, block, tuple(coefs), unroll=4)

    loads["res"].wait()

    def make_taps(t, _):
        cols = lanes_of(t)
        rate = dec[:, cols]
        weight = res[:, cols]
        step = jnp.exp(rate * (-float(sub)))
        steps = [spread(step, n) for n in range(modes)]
        coefs = [spread(weight, n) * jnp.exp(-spread(rate, n) * sublane) for n in range(modes)]

        def emit(at, value):
            taps[at, cols] = value.astype(bf16)

        modal(coefs, steps, emit)
        return 0

    lax.fori_loop(0, n_lane, make_taps, 0)

    for d, copy in enumerate(first, 1):
        pltpu.make_async_remote_copy(
            src_ref=ends.at[mine], dst_ref=got.at[lax.rem(me - d + n_ctx, n_ctx)],
            send_sem=send1.at[d], recv_sem=recv1.at[d], device_id={"ctx": me}, device_id_type=MESH,
        ).wait_recv()
    got[me] = ends[mine]
    power = decay_pow[mine]
    running = jnp.zeros_like(power)
    for j in range(n_ctx):
        starts[j] = running
        running = running * power + got[j]

    second = []
    for d in range(1, n_ctx):
        to = lax.rem(me + d, n_ctx)
        copy = pltpu.make_async_remote_copy(
            src_ref=starts.at[to], dst_ref=states.at[mine],
            send_sem=send2.at[d], recv_sem=recv2.at[d], device_id={"ctx": to}, device_id_type=MESH,
        )
        copy.start()
        second.append(copy)
    states[mine] = starts[me]

    loads["fwd"].wait()
    loads["inv"].wait()

    def local_conv(c, _):
        cols = pl.ds(pl.multiple_of(c * dft_cols, dft_cols), dft_cols)
        u = jnp.dot(fwd[...], sig[:, cols], preferred_element_type=f32)
        h = jnp.dot(fwd[...], taps[:, cols], preferred_element_type=f32)
        ur, ui, hr, hi = u[:rows], u[rows:], h[:rows], h[rows:]
        prod = jnp.concatenate([ur * hr - ui * hi, ur * hi + ui * hr], axis=0).astype(bf16)
        conv[:, cols] = jnp.dot(inv[...], prod, preferred_element_type=f32)
        return 0

    lax.fori_loop(0, width // dft_cols, local_conv, 0)

    for name in ("v", "stream", "skip", "gain"):
        loads[name].wait()
    square[...] = jnp.zeros_like(square)

    for d in range(1, n_ctx):
        frm = lax.rem(me - d + n_ctx, n_ctx)
        pltpu.make_async_remote_copy(
            src_ref=starts.at[me], dst_ref=states.at[pl.ds(frm * per_dev, per_dev)],
            send_sem=send2.at[d], recv_sem=recv2.at[d], device_id={"ctx": me}, device_id_type=MESH,
        ).wait_recv()

    def finish(t, _):
        cols = lanes_of(t)
        rate = dec[:, cols]
        state = jnp.concatenate([states[t * n_sub + g] for g in range(n_sub)], axis=0)
        weight = res[:, cols] * state
        step = jnp.exp(rate * (-float(sub)))
        steps = [spread(step, n) for n in range(modes)]
        coefs = [spread(weight, n) * jnp.exp(-spread(rate, n) * (sublane + 1.0)) for n in range(modes)]
        direct = skip[:, cols]

        def emit(at, value):
            value = value + conv[at, cols] + direct * sig[at, cols].astype(f32)
            out = (stream[at, cols].astype(f32) + v[at, cols].astype(f32) * value).astype(bf16)
            new[at, cols] = out
            out = out.astype(f32)
            square[at, :] += out * out

        modal(coefs, steps, emit)
        return 0

    lax.fori_loop(0, n_lane, finish, 0)
    write_new = pltpu.make_async_copy(new, new_hbm, out_sem.at[0])
    write_new.start()

    ones = jnp.ones((sub, lane), f32)
    row_sums[tp] = lax.dot_general(
        ones, square[...], (((1,), (1,)), ((), ())),
        precision=lax.Precision.HIGHEST, preferred_element_type=f32,
    )
    third = []
    for d in range(1, n_tp):
        to = lax.rem(tp + d, n_tp)
        copy = pltpu.make_async_remote_copy(
            src_ref=row_sums.at[tp], dst_ref=row_sums.at[tp],
            send_sem=send3.at[d], recv_sem=recv3.at[d], device_id={"tp": to}, device_id_type=MESH,
        )
        copy.start()
        third.append(copy)
    for d in range(1, n_tp):
        frm = lax.rem(tp - d + n_tp, n_tp)
        pltpu.make_async_remote_copy(
            src_ref=row_sums.at[tp], dst_ref=row_sums.at[frm],
            send_sem=send3.at[d], recv_sem=recv3.at[d], device_id={"tp": tp}, device_id_type=MESH,
        ).wait_recv()
    total = row_sums[0]
    for j in range(1, n_tp):
        total = total + row_sums[j]
    mean = lax.dot_general(
        total, jnp.full((sub, lane), 1.0 / sub, f32), (((0,), (0,)), ((), ())),
        precision=lax.Precision.HIGHEST, preferred_element_type=f32,
    ) / (width * n_tp)
    square[...] = lax.rsqrt(mean + epsilon)

    def scale(t, _):
        cols = lanes_of(t)
        norm[:, cols] = (new[:, cols].astype(f32) * square[...] * gain[:, cols]).astype(bf16)
        return 0

    lax.fori_loop(0, n_lane, scale, 0)
    write_norm = pltpu.make_async_copy(norm, norm_hbm, out_sem.at[1])
    write_norm.start()
    for copy in first + second + third:
        copy.wait_send()
    write_new.wait()
    write_norm.wait()


def shards(n_ctx, n_tp, queries, key_proj, values, residues, decay_rates, skip_weight, stream, norm_gain):
    rows, width = queries.shape
    modes = residues.shape[0]
    n_lane = width // lane
    n_sub = max(1, n_ctx // n_lane)
    part = modes // n_sub
    blocks = n_lane * n_sub
    per_dev = blocks // n_ctx
    assert per_dev * n_ctx == blocks and part * n_sub == modes
    forward, inverse = dft_tables(rows)
    slab = pltpu.VMEM((rows, width), bf16)
    wide = pltpu.VMEM((modes, width), f32)
    line = pltpu.VMEM((1, width), f32)
    dma = pltpu.SemaphoreType.DMA
    whole = pl.BlockSpec(memory_space=pl.ANY)
    out = jax.ShapeDtypeStruct((rows, width), bf16)
    return pl.pallas_call(
        functools.partial(body, n_ctx, n_tp, n_sub, per_dev),
        out_shape=(out, out),
        in_specs=[whole] * 10,
        out_specs=(whole, whole),
        scratch_shapes=[
            slab, slab, slab, wide, wide, line, slab, line,
            pltpu.VMEM((2 * rows, rows), bf16), pltpu.VMEM((rows, 2 * rows), bf16),
            slab, slab, pltpu.VMEM((rows, width), f32), slab, slab,
            pltpu.VMEM((blocks, part, lane), f32),
            pltpu.VMEM((blocks, part, lane), f32),
            pltpu.VMEM((n_ctx, per_dev, part, lane), f32),
            pltpu.VMEM((n_ctx, per_dev, part, lane), f32),
            pltpu.VMEM((blocks, part, lane), f32),
            pltpu.VMEM((rows, lane), f32),
            pltpu.VMEM((n_tp, sub, rows), f32),
            dma((10,)), dma((2,)),
            dma((n_ctx,)), dma((n_ctx,)), dma((n_ctx,)), dma((n_ctx,)), dma((n_tp,)), dma((n_tp,)),
        ],
        compiler_params=pltpu.CompilerParams(
            collective_id=0, has_side_effects=True, vmem_limit_bytes=48 * 1024 * 1024
        ),
        cost_estimate=pl.CostEstimate(
            flops=6 * rows * rows * width * 2, bytes_accessed=6 * rows * width * 2, transcendentals=0
        ),
    )(
        queries, key_proj, values, residues, decay_rates, skip_weight[None, :], stream,
        norm_gain[None, :], jnp.asarray(forward), jnp.asarray(inverse),
    )


def solution(mesh):
    in_specs = (
        P("ctx", "tp"),
        P("ctx", "tp"),
        P("ctx", "tp"),
        P(None, "tp"),
        P(None, "tp"),
        P("tp"),
        P("ctx", "tp"),
        P("tp"),
    )
    out_specs = (P("ctx", "tp"), P("ctx", "tp"))
    return jax.shard_map(
        functools.partial(shards, mesh.shape["ctx"], mesh.shape["tp"]),
        mesh=mesh, in_specs=in_specs, out_specs=out_specs, check_vma=False,
    )
```

```python
import functools
import math

import jax
import jax.numpy as jnp
import numpy as np
from jax import lax
from jax.experimental import pallas as pl
from jax.experimental.pallas import tpu as pltpu
from jax.sharding import PartitionSpec as P

epsilon = 1e-06
lane = 128
sub = 8
dft_cols = 256
MESH = pl.DeviceIdType.MESH
f32 = jnp.float32
bf16 = jnp.bfloat16


def dft_tables(rows):
    freq = np.arange(rows)[:, None]
    pos = np.arange(rows)[None, :]
    angle = math.pi * (((2 * freq + 1) * pos) % (4 * rows)) / (2 * rows)
    forward = np.concatenate([np.cos(angle), -np.sin(angle)], axis=0)
    inverse = np.concatenate([np.cos(angle).T, -np.sin(angle).T], axis=1) / rows
    return np.ascontiguousarray(forward.astype(bf16)), np.ascontiguousarray(inverse.astype(bf16))


def body(
    n_ctx, n_tp, n_sub, per_dev, chunk,
    q_hbm, k_hbm, v_hbm, res_hbm, dec_hbm, skip_hbm, str_hbm, fwd_hbm, inv_hbm,
    new, inv_rms,
    q, k, v, res, dec, skip, stream, fwd, inv,
    sig, taps, conv, ends, mids, decay_pow, got, starts, states, square, row_sums,
    in_sem, send1, recv1, send2, recv2, send3, recv3,
):
    rows, width = q.shape
    modes = res.shape[0]
    n_lane = width // lane
    n_chunk = rows // chunk
    part = modes // n_sub
    me = lax.axis_index("ctx")
    tp = lax.axis_index("tp")

    loads = {}
    order = [
        ("dec", dec_hbm, dec), ("q", q_hbm, q), ("k", k_hbm, k), ("res", res_hbm, res),
        ("fwd", fwd_hbm, fwd), ("inv", inv_hbm, inv), ("v", v_hbm, v),
        ("stream", str_hbm, stream), ("skip", skip_hbm, skip),
    ]
    for i, (name, src, dst) in enumerate(order):
        loads[name] = pltpu.make_async_copy(src, dst, in_sem.at[i])
        loads[name].start()

    barrier = pltpu.get_barrier_semaphore()
    for d in range(1, n_ctx):
        pl.semaphore_signal(barrier, inc=1, device_id={"ctx": lax.rem(me + d, n_ctx)}, device_id_type=MESH)
    for d in range(1, n_tp):
        pl.semaphore_signal(barrier, inc=1, device_id={"tp": lax.rem(tp + d, n_tp)}, device_id_type=MESH)

    sublane = lax.broadcasted_iota(jnp.int32, (sub, lane), 0).astype(f32)

    def lanes_of(t):
        return pl.ds(pl.multiple_of(t * lane, lane), lane)

    def spread(x, n):
        return jnp.broadcast_to(x[n:n + 1, :], (sub, lane))

    def rows_of(h, m):
        return pl.ds(pl.multiple_of(h * chunk + m * 16, 16), 16)

    for name in ("dec", "q", "k"):
        loads[name].wait()

    def end_states(t):
        cols = lanes_of(t)
        rate = dec[:, cols]
        step = jnp.exp(rate * (-float(sub)))
        steps = [spread(step, n) for n in range(modes)]
        tails = [jnp.exp(-spread(rate, n) * (sub - 1.0 - sublane)) for n in range(modes)]
        acc = (jnp.zeros((sub, lane), f32),) * modes
        for h in range(n_chunk):

            def block(m, acc):
                at = rows_of(h, m)
                s = (q[at, cols].astype(f32) * k[at, cols].astype(f32)).astype(bf16)
                sig[at, cols] = s
                s = s.astype(f32)
                acc = tuple(a * b + s[:8] for a, b in zip(acc, steps))
                return tuple(a * b + s[8:] for a, b in zip(acc, steps))

            acc = lax.fori_loop(0, chunk // 16, block, acc, unroll=True)
            total = jnp.concatenate(
                [jnp.sum(a * w, axis=0, keepdims=True) for a, w in zip(acc, tails)], axis=0
            )
            if h < n_chunk - 1:
                mids[h, t] = total
        power = jnp.exp(rate * (-float(rows)))
        for g in range(n_sub):
            ends[t * n_sub + g] = total[g * part:(g + 1) * part]
            decay_pow[t * n_sub + g] = power[g * part:(g + 1) * part]

    def loop(first, last, step):
        def run(i, _):
            step(i)
            return 0

        lax.fori_loop(first, last, run, 0)

    mine = pl.ds(me * per_dev, per_dev)

    def copy_ends(d):
        to = lax.rem(me + d, n_ctx)
        return pltpu.make_async_remote_copy(
            src_ref=ends.at[pl.ds(to * per_dev, per_dev)], dst_ref=got.at[me],
            send_sem=send1.at[d], recv_sem=recv1.at[d], device_id={"ctx": to}, device_id_type=MESH,
        )

    if n_sub == 1:
        def share(d):
            loop(0, per_dev, lambda i: end_states(lax.rem(me + d, n_ctx) * per_dev + i))

        share(1)
        pl.semaphore_wait(barrier, n_ctx - 1 + n_tp - 1)
        copy_ends(1).start()

        def share_and_send(d):
            share(d)
            copy_ends(d).start()

        loop(2, n_ctx, share_and_send)
        share(0)
    else:
        loop(0, n_lane, end_states)
        pl.semaphore_wait(barrier, n_ctx - 1 + n_tp - 1)
        loop(1, n_ctx, lambda d: copy_ends(d).start())

    def modal(h, coefs, steps, emit):
        def block(m, z):
            top = sum(z[1:], z[0])
            z = tuple(a * b for a, b in zip(z, steps))
            low = sum(z[1:], z[0])
            z = tuple(a * b for a, b in zip(z, steps))
            emit(rows_of(h, m), jnp.concatenate([top, low], axis=0))
            return z

        lax.fori_loop(0, chunk // 16, block, tuple(coefs), unroll=True)

    loads["res"].wait()

    def make_taps(t):
        cols = lanes_of(t)
        rate = dec[:, cols]
        weight = res[:, cols]
        step = jnp.exp(rate * (-float(sub)))
        steps = [spread(step, n) for n in range(modes)]
        coefs = [spread(weight, n) * jnp.exp(-spread(rate, n) * sublane) for n in range(modes)]

        def emit(at, value):
            taps[at, cols] = value.astype(bf16)

        modal(0, coefs, steps, emit)

    loop(0, n_lane, make_taps)

    loop(1, n_ctx, lambda d: copy_ends(d).wait_recv())
    got[me] = ends[mine]
    power = decay_pow[mine]
    running = jnp.zeros_like(power)
    for j in range(n_ctx):
        starts[j] = running
        running = running * power + got[j]

    def copy_starts(d):
        to = lax.rem(me + d, n_ctx)
        return pltpu.make_async_remote_copy(
            src_ref=starts.at[to], dst_ref=states.at[mine],
            send_sem=send2.at[d], recv_sem=recv2.at[d], device_id={"ctx": to}, device_id_type=MESH,
        )

    loop(1, n_ctx, lambda d: copy_starts(d).start())
    states[mine] = starts[me]

    loads["fwd"].wait()
    loads["inv"].wait()

    def local_conv(c):
        cols = pl.ds(pl.multiple_of(c * dft_cols, dft_cols), dft_cols)
        g = jnp.dot(fwd[...], taps[:, cols], preferred_element_type=f32)
        gr, gi = g[:chunk], g[chunk:]
        for h in range(n_chunk):
            at = pl.ds(h * chunk, chunk)
            u = jnp.dot(fwd[...], sig[at, cols], preferred_element_type=f32)
            ur, ui = u[:chunk], u[chunk:]
            prod = jnp.concatenate([ur * gr - ui * gi, ur * gi + ui * gr], axis=0).astype(bf16)
            conv[at, cols] = jnp.dot(inv[...], prod, preferred_element_type=f32)

    loop(0, width // dft_cols, local_conv)

    for name in ("v", "stream", "skip"):
        loads[name].wait()
    square[...] = jnp.zeros_like(square)

    def finish(t):
        cols = lanes_of(t)
        rate = dec[:, cols]
        state = jnp.concatenate([states[t * n_sub + g] for g in range(n_sub)], axis=0)
        weight = res[:, cols]
        step = jnp.exp(rate * (-float(sub)))
        steps = [spread(step, n) for n in range(modes)]
        heads = [jnp.exp(-spread(rate, n) * (sublane + 1.0)) for n in range(modes)]
        direct = skip[:, cols]

        def emit(at, value):
            value = value + conv[at, cols] + direct * sig[at, cols].astype(f32)
            out = (stream[at, cols].astype(f32) + v[at, cols].astype(f32) * value).astype(bf16)
            new[at, cols] = out
            out = out.astype(f32)
            square[at, :] += out * out

        for h in range(n_chunk):
            now = state if h == 0 else state * jnp.exp(rate * (-float(h * chunk))) + mids[h - 1, t]
            now = now * weight
            modal(h, [spread(now, n) * w for n, w in enumerate(heads)], steps, emit)

    if n_sub == 1:
        def finish_share(d):
            frm = lax.rem(me - d + n_ctx, n_ctx)
            loop(0, per_dev, lambda i: finish(frm * per_dev + i))

        def wait_and_finish(d):
            frm = lax.rem(me - d + n_ctx, n_ctx)
            pltpu.make_async_remote_copy(
                src_ref=starts.at[me], dst_ref=states.at[pl.ds(frm * per_dev, per_dev)],
                send_sem=send2.at[d], recv_sem=recv2.at[d], device_id={"ctx": frm}, device_id_type=MESH,
            ).wait_recv()
            finish_share(d)

        finish_share(0)
        loop(1, n_ctx, wait_and_finish)
    else:
        loop(1, n_ctx, lambda d: copy_starts(d).wait_recv())
        loop(0, n_lane, finish)

    ones = jnp.ones((sub, lane), f32)
    row_sums[tp] = lax.dot_general(
        ones, square[...], (((1,), (1,)), ((), ())),
        precision=lax.Precision.HIGHEST, preferred_element_type=f32,
    )
    third = []
    for d in range(1, n_tp):
        to = lax.rem(tp + d, n_tp)
        copy = pltpu.make_async_remote_copy(
            src_ref=row_sums.at[tp], dst_ref=row_sums.at[tp],
            send_sem=send3.at[d], recv_sem=recv3.at[d], device_id={"tp": to}, device_id_type=MESH,
        )
        copy.start()
        third.append(copy)
    loop(1, n_ctx, lambda d: copy_ends(d).wait_send())
    loop(1, n_ctx, lambda d: copy_starts(d).wait_send())
    for copy in third:
        copy.wait_recv()
    total = row_sums[0]
    for j in range(1, n_tp):
        total = total + row_sums[j]
    mean = lax.dot_general(
        total, jnp.full((sub, lane), 1.0 / sub, f32), (((0,), (0,)), ((), ())),
        precision=lax.Precision.HIGHEST, preferred_element_type=f32,
    ) / (width * n_tp)
    inv_rms[...] = lax.rsqrt(mean + epsilon)
    for copy in third:
        copy.wait_send()


def scale_body(new, inv_rms, gain, new_hbm, norm_hbm, norm, sems):
    rows, width = new.shape
    writes = [pltpu.make_async_copy(new, new_hbm, sems.at[0])]
    writes[0].start()
    piece = rows // 4
    for p in range(4):
        at = pl.ds(p * piece, piece)
        factor = inv_rms[at, :]

        def scale(t, _):
            cols = pl.ds(pl.multiple_of(t * lane, lane), lane)
            norm[at, cols] = (new[at, cols].astype(f32) * factor * gain[:, cols]).astype(bf16)
            return 0

        lax.fori_loop(0, width // lane, scale, 0, unroll=4)
        writes.append(pltpu.make_async_copy(norm.at[at], norm_hbm.at[at], sems.at[p + 1]))
        writes[-1].start()
    for write in writes:
        write.wait()


def shards(n_ctx, n_tp, queries, key_proj, values, residues, decay_rates, skip_weight, stream, norm_gain):
    rows, width = queries.shape
    modes = residues.shape[0]
    n_lane = width // lane
    n_sub = max(1, n_ctx // n_lane)
    part = modes // n_sub
    blocks = n_lane * n_sub
    per_dev = blocks // n_ctx
    chunk = rows // 2
    assert per_dev * n_ctx == blocks and part * n_sub == modes
    forward, inverse = dft_tables(chunk)
    slab = pltpu.VMEM((rows, width), bf16)
    wide = pltpu.VMEM((modes, width), f32)
    line = pltpu.VMEM((1, width), f32)
    dma = pltpu.SemaphoreType.DMA
    whole = pl.BlockSpec(memory_space=pl.ANY)
    near = pl.BlockSpec(memory_space=pltpu.VMEM)
    out = jax.ShapeDtypeStruct((rows, width), bf16)
    args = (
        queries, key_proj, values, residues, decay_rates, skip_weight[None, :], stream,
        jnp.asarray(forward), jnp.asarray(inverse),
    )
    new, inv_rms = pl.pallas_call(
        functools.partial(body, n_ctx, n_tp, n_sub, per_dev, chunk),
        out_shape=(pltpu.VMEM((rows, width), bf16), pltpu.VMEM((rows, lane), f32)),
        in_specs=[whole] * 9,
        out_specs=(near, near),
        scratch_shapes=[
            slab, slab, slab, wide, wide, line, slab,
            pltpu.VMEM((2 * chunk, chunk), bf16), pltpu.VMEM((chunk, 2 * chunk), bf16),
            slab, pltpu.VMEM((chunk, width), bf16), pltpu.VMEM((rows, width), f32),
            pltpu.VMEM((blocks, part, lane), f32),
            pltpu.VMEM((rows // chunk - 1, n_lane, modes, lane), f32),
            pltpu.VMEM((blocks, part, lane), f32),
            pltpu.VMEM((n_ctx, per_dev, part, lane), f32),
            pltpu.VMEM((n_ctx, per_dev, part, lane), f32),
            pltpu.VMEM((blocks, part, lane), f32),
            pltpu.VMEM((rows, lane), f32),
            pltpu.VMEM((n_tp, sub, rows), f32),
            dma((9,)),
            dma((n_ctx,)), dma((n_ctx,)), dma((n_ctx,)), dma((n_ctx,)), dma((n_tp,)), dma((n_tp,)),
        ],
        compiler_params=pltpu.CompilerParams(
            collective_id=0, has_side_effects=True, vmem_limit_bytes=40 * 1024 * 1024
        ),
        cost_estimate=pl.CostEstimate(
            flops=6 * rows * rows * width * 2, bytes_accessed=6 * rows * width * 2, transcendentals=0
        ),
    )(*[pltpu.with_memory_space_constraint(x, pltpu.HBM) for x in args])
    return pl.pallas_call(
        scale_body,
        out_shape=(out, out),
        in_specs=[near] * 3,
        out_specs=(whole, whole),
        scratch_shapes=[slab, dma((5,))],
        compiler_params=pltpu.CompilerParams(vmem_limit_bytes=40 * 1024 * 1024),
        cost_estimate=pl.CostEstimate(flops=2 * rows * width, bytes_accessed=6 * rows * width, transcendentals=0),
    )(new, inv_rms, norm_gain[None, :])


def solution(mesh):
    in_specs = (
        P("ctx", "tp"),
        P("ctx", "tp"),
        P("ctx", "tp"),
        P(None, "tp"),
        P(None, "tp"),
        P("tp"),
        P("ctx", "tp"),
        P("tp"),
    )
    out_specs = (P("ctx", "tp"), P("ctx", "tp"))
    return jax.shard_map(
        functools.partial(shards, mesh.shape["ctx"], mesh.shape["tp"]),
        mesh=mesh, in_specs=in_specs, out_specs=out_specs, check_vma=False,
    )
```

```python
import functools
import math

import jax
import jax.numpy as jnp
import numpy as np
from jax import lax
from jax.experimental import pallas as pl
from jax.experimental.pallas import tpu as pltpu
from jax.sharding import PartitionSpec as P

epsilon = 1e-06
lane = 128
sub = 8
dft_cols = 256
MESH = pl.DeviceIdType.MESH
f32 = jnp.float32
bf16 = jnp.bfloat16


def tree_sum(terms):
    while len(terms) > 1:
        terms = [a + b for a, b in zip(terms[::2], terms[1::2])] + terms[len(terms) // 2 * 2:]
    return terms[0]


def dft_tables(rows):
    freq = np.arange(rows)[:, None]
    pos = np.arange(rows)[None, :]
    angle = math.pi * (((2 * freq + 1) * pos) % (4 * rows)) / (2 * rows)
    forward = np.concatenate([np.cos(angle), -np.sin(angle)], axis=0)
    inverse = np.concatenate([np.cos(angle).T, -np.sin(angle).T], axis=0) / rows
    return np.ascontiguousarray(forward.astype(bf16)), np.ascontiguousarray(inverse.astype(bf16))


def body(
    n_ctx, n_tp, n_sub, per_dev, chunk,
    q_hbm, k_hbm, v_hbm, res_hbm, dec_hbm, skip_hbm, str_hbm, fwd_hbm, inv_hbm,
    new, inv_rms,
    q, k, v, res, dec, skip, stream, fwd, inv,
    sig, taps, conv, ends, mids, decay_pow, got, starts, states, square, row_sums,
    in_sem, send1, recv1, send2, recv2, send3, recv3,
):
    rows, width = q.shape
    modes = res.shape[0]
    n_lane = width // lane
    n_chunk = rows // chunk
    part = modes // n_sub
    me = lax.axis_index("ctx")
    tp = lax.axis_index("tp")

    loads = {}
    order = [
        ("dec", dec_hbm, dec), ("q", q_hbm, q), ("k", k_hbm, k), ("res", res_hbm, res),
        ("fwd", fwd_hbm, fwd), ("inv", inv_hbm, inv), ("v", v_hbm, v),
        ("stream", str_hbm, stream), ("skip", skip_hbm, skip),
    ]
    for i, (name, src, dst) in enumerate(order):
        loads[name] = pltpu.make_async_copy(src, dst, in_sem.at[i])
        loads[name].start()

    barrier = pltpu.get_barrier_semaphore()
    for d in range(1, n_ctx):
        pl.semaphore_signal(barrier, inc=1, device_id={"ctx": lax.rem(me + d, n_ctx)}, device_id_type=MESH)
    for d in range(1, n_tp):
        pl.semaphore_signal(barrier, inc=1, device_id={"tp": lax.rem(tp + d, n_tp)}, device_id_type=MESH)

    sublane = lax.broadcasted_iota(jnp.int32, (sub, lane), 0).astype(f32)

    def lanes_of(t):
        return pl.ds(pl.multiple_of(t * lane, lane), lane)

    def spread(x, n):
        return jnp.broadcast_to(x[n:n + 1, :], (sub, lane))

    def rows_of(h, m):
        return pl.ds(pl.multiple_of(h * chunk + m * 16, 16), 16)

    for name in ("dec", "q", "k"):
        loads[name].wait()

    def end_states(t):
        cols = lanes_of(t)
        rate = dec[:, cols]
        step = jnp.exp(rate * (-float(sub)))
        steps = [spread(step, n) for n in range(modes)]
        tails = [jnp.exp(-spread(rate, n) * (sub - 1.0 - sublane)) for n in range(modes)]
        acc = (jnp.zeros((sub, lane), f32),) * modes
        for h in range(n_chunk):

            def block(m, acc):
                at = rows_of(h, m)
                s = (q[at, cols].astype(f32) * k[at, cols].astype(f32)).astype(bf16)
                sig[at, cols] = s
                s = s.astype(f32)
                acc = tuple(a * b + s[:8] for a, b in zip(acc, steps))
                return tuple(a * b + s[8:] for a, b in zip(acc, steps))

            acc = lax.fori_loop(0, chunk // 16, block, acc, unroll=True)
            total = jnp.concatenate(
                [jnp.sum(a * w, axis=0, keepdims=True) for a, w in zip(acc, tails)], axis=0
            )
            if h < n_chunk - 1:
                mids[h, t] = total
        power = jnp.exp(rate * (-float(rows)))
        for g in range(n_sub):
            ends[t * n_sub + g] = total[g * part:(g + 1) * part]
            decay_pow[t * n_sub + g] = power[g * part:(g + 1) * part]

    def loop(first, last, step):
        def run(i, _):
            step(i)
            return 0

        lax.fori_loop(first, last, run, 0)

    mine = pl.ds(me * per_dev, per_dev)

    def copy_ends(d):
        to = lax.rem(me + d, n_ctx)
        return pltpu.make_async_remote_copy(
            src_ref=ends.at[pl.ds(to * per_dev, per_dev)], dst_ref=got.at[me],
            send_sem=send1.at[d], recv_sem=recv1.at[d], device_id={"ctx": to}, device_id_type=MESH,
        )

    if n_sub == 1:
        def share(d):
            loop(0, per_dev, lambda i: end_states(lax.rem(me + d, n_ctx) * per_dev + i))

        share(1)
        pl.semaphore_wait(barrier, n_ctx - 1 + n_tp - 1)
        copy_ends(1).start()

        def share_and_send(d):
            share(d)
            copy_ends(d).start()

        loop(2, n_ctx, share_and_send)
        share(0)
    else:
        loop(0, n_lane, end_states)
        pl.semaphore_wait(barrier, n_ctx - 1 + n_tp - 1)
        loop(1, n_ctx, lambda d: copy_ends(d).start())

    def modal(h, coefs, steps, emit):
        def block(m, z):
            top = tree_sum(list(z))
            z = tuple(a * b for a, b in zip(z, steps))
            low = tree_sum(list(z))
            z = tuple(a * b for a, b in zip(z, steps))
            emit(rows_of(h, m), jnp.concatenate([top, low], axis=0))
            return z

        lax.fori_loop(0, chunk // 16, block, tuple(coefs), unroll=True)

    for name in ("res", "fwd", "inv", "v", "stream", "skip"):
        loads[name].wait()

    def local_part(c):
        for i in range(dft_cols // lane):
            cols = lanes_of(c * (dft_cols // lane) + i)
            rate = dec[:, cols]
            weight = res[:, cols]
            step = jnp.exp(rate * (-float(sub)))
            steps = [spread(step, n) for n in range(modes)]
            coefs = [spread(weight, n) * jnp.exp(-spread(rate, n) * sublane) for n in range(modes)]

            def emit(at, value):
                taps[at, i * lane:(i + 1) * lane] = value.astype(bf16)

            modal(0, coefs, steps, emit)

        cols = pl.ds(pl.multiple_of(c * dft_cols, dft_cols), dft_cols)
        table = fwd[...]
        back = jnp.concatenate([inv[:chunk, :], inv[chunk:, :]], axis=1)
        g = jnp.dot(table, taps[...], preferred_element_type=f32)
        gr, gi = g[:chunk], g[chunk:]
        direct = skip[:, cols]
        for h in range(n_chunk):
            at = pl.ds(h * chunk, chunk)
            part_sig = sig[at, cols]
            u = jnp.dot(table, part_sig, preferred_element_type=f32)
            ur, ui = u[:chunk], u[chunk:]
            prod = jnp.concatenate([ur * gr - ui * gi, ur * gi + ui * gr], axis=0).astype(bf16)
            value = jnp.dot(back, prod, preferred_element_type=f32) + direct * part_sig.astype(f32)
            conv[at, cols] = stream[at, cols].astype(f32) + v[at, cols].astype(f32) * value

    n_local = width // dft_cols
    loop(0, n_local // 2, local_part)

    loop(1, n_ctx, lambda d: copy_ends(d).wait_recv())
    got[me] = ends[mine]
    power = decay_pow[mine]
    running = jnp.zeros_like(power)
    for j in range(n_ctx):
        starts[j] = running
        running = running * power + got[j]

    def copy_starts(d):
        to = lax.rem(me + d, n_ctx)
        return pltpu.make_async_remote_copy(
            src_ref=starts.at[to], dst_ref=states.at[mine],
            send_sem=send2.at[d], recv_sem=recv2.at[d], device_id={"ctx": to}, device_id_type=MESH,
        )

    loop(1, n_ctx, lambda d: copy_starts(d).start())
    states[mine] = starts[me]

    loop(n_local // 2, n_local, local_part)

    square[...] = jnp.zeros_like(square)

    def finish(t):
        cols = lanes_of(t)
        rate = dec[:, cols]
        state = jnp.concatenate([states[t * n_sub + g] for g in range(n_sub)], axis=0)
        weight = res[:, cols]
        step = jnp.exp(rate * (-float(sub)))
        steps = [spread(step, n) for n in range(modes)]
        heads = [jnp.exp(-spread(rate, n) * (sublane + 1.0)) for n in range(modes)]

        def emit(at, value):
            out = (conv[at, cols] + v[at, cols].astype(f32) * value).astype(bf16)
            new[at, cols] = out
            out = out.astype(f32)
            square[at, :] += out * out

        for h in range(n_chunk):
            now = state if h == 0 else state * jnp.exp(rate * (-float(h * chunk))) + mids[h - 1, t]
            now = now * weight
            modal(h, [spread(now, n) * w for n, w in enumerate(heads)], steps, emit)

    if n_sub == 1:
        def finish_share(d):
            frm = lax.rem(me - d + n_ctx, n_ctx)
            loop(0, per_dev, lambda i: finish(frm * per_dev + i))

        def wait_and_finish(d):
            frm = lax.rem(me - d + n_ctx, n_ctx)
            pltpu.make_async_remote_copy(
                src_ref=starts.at[me], dst_ref=states.at[pl.ds(frm * per_dev, per_dev)],
                send_sem=send2.at[d], recv_sem=recv2.at[d], device_id={"ctx": frm}, device_id_type=MESH,
            ).wait_recv()
            finish_share(d)

        finish_share(0)
        loop(1, n_ctx, wait_and_finish)
    else:
        loop(1, n_ctx, lambda d: copy_starts(d).wait_recv())
        loop(0, n_lane, finish)

    ones = jnp.ones((sub, lane), f32)
    row_sums[tp] = lax.dot_general(
        ones, square[...], (((1,), (1,)), ((), ())),
        precision=lax.Precision.HIGHEST, preferred_element_type=f32,
    )
    third = []
    for d in range(1, n_tp):
        to = lax.rem(tp + d, n_tp)
        copy = pltpu.make_async_remote_copy(
            src_ref=row_sums.at[tp], dst_ref=row_sums.at[tp],
            send_sem=send3.at[d], recv_sem=recv3.at[d], device_id={"tp": to}, device_id_type=MESH,
        )
        copy.start()
        third.append(copy)
    loop(1, n_ctx, lambda d: copy_ends(d).wait_send())
    loop(1, n_ctx, lambda d: copy_starts(d).wait_send())
    for copy in third:
        copy.wait_recv()
    total = row_sums[0]
    for j in range(1, n_tp):
        total = total + row_sums[j]
    mean = lax.dot_general(
        total, jnp.full((sub, lane), 1.0 / sub, f32), (((0,), (0,)), ((), ())),
        precision=lax.Precision.HIGHEST, preferred_element_type=f32,
    ) / (width * n_tp)
    inv_rms[...] = lax.rsqrt(mean + epsilon)
    for copy in third:
        copy.wait_send()


def scale_body(new, inv_rms, gain, new_hbm, norm_hbm, norm, sems):
    rows, width = new.shape
    writes = [pltpu.make_async_copy(new, new_hbm, sems.at[0])]
    writes[0].start()
    piece = rows // 4
    for p in range(4):
        at = pl.ds(p * piece, piece)
        factor = inv_rms[at, :]

        def scale(t, _):
            cols = pl.ds(pl.multiple_of(t * lane, lane), lane)
            norm[at, cols] = (new[at, cols].astype(f32) * factor * gain[:, cols]).astype(bf16)
            return 0

        lax.fori_loop(0, width // lane, scale, 0, unroll=4)
        writes.append(pltpu.make_async_copy(norm.at[at], norm_hbm.at[at], sems.at[p + 1]))
        writes[-1].start()
    for write in writes:
        write.wait()


def shards(n_ctx, n_tp, queries, key_proj, values, residues, decay_rates, skip_weight, stream, norm_gain):
    rows, width = queries.shape
    modes = residues.shape[0]
    n_lane = width // lane
    n_sub = max(1, n_ctx // n_lane)
    part = modes // n_sub
    blocks = n_lane * n_sub
    per_dev = blocks // n_ctx
    chunk = rows // 2
    assert per_dev * n_ctx == blocks and part * n_sub == modes
    forward, inverse = dft_tables(chunk)
    slab = pltpu.VMEM((rows, width), bf16)
    wide = pltpu.VMEM((modes, width), f32)
    line = pltpu.VMEM((1, width), f32)
    dma = pltpu.SemaphoreType.DMA
    whole = pl.BlockSpec(memory_space=pl.ANY)
    near = pl.BlockSpec(memory_space=pltpu.VMEM)
    out = jax.ShapeDtypeStruct((rows, width), bf16)
    args = (
        queries, key_proj, values, residues, decay_rates, skip_weight[None, :], stream,
        jnp.asarray(forward), jnp.asarray(inverse),
    )
    new, inv_rms = pl.pallas_call(
        functools.partial(body, n_ctx, n_tp, n_sub, per_dev, chunk),
        out_shape=(pltpu.VMEM((rows, width), bf16), pltpu.VMEM((rows, lane), f32)),
        in_specs=[whole] * 9,
        out_specs=(near, near),
        scratch_shapes=[
            slab, slab, slab, wide, wide, line, slab,
            pltpu.VMEM((2 * chunk, chunk), bf16), pltpu.VMEM((2 * chunk, chunk), bf16),
            slab, pltpu.VMEM((chunk, dft_cols), bf16), pltpu.VMEM((rows, width), f32),
            pltpu.VMEM((blocks, part, lane), f32),
            pltpu.VMEM((rows // chunk - 1, n_lane, modes, lane), f32),
            pltpu.VMEM((blocks, part, lane), f32),
            pltpu.VMEM((n_ctx, per_dev, part, lane), f32),
            pltpu.VMEM((n_ctx, per_dev, part, lane), f32),
            pltpu.VMEM((blocks, part, lane), f32),
            pltpu.VMEM((rows, lane), f32),
            pltpu.VMEM((n_tp, sub, rows), f32),
            dma((9,)),
            dma((n_ctx,)), dma((n_ctx,)), dma((n_ctx,)), dma((n_ctx,)), dma((n_tp,)), dma((n_tp,)),
        ],
        compiler_params=pltpu.CompilerParams(
            collective_id=0, has_side_effects=True, vmem_limit_bytes=40 * 1024 * 1024
        ),
        cost_estimate=pl.CostEstimate(
            flops=6 * rows * rows * width * 2, bytes_accessed=6 * rows * width * 2, transcendentals=0
        ),
    )(*[pltpu.with_memory_space_constraint(x, pltpu.HBM) for x in args])
    return pl.pallas_call(
        scale_body,
        out_shape=(out, out),
        in_specs=[near] * 3,
        out_specs=(whole, whole),
        scratch_shapes=[slab, dma((5,))],
        compiler_params=pltpu.CompilerParams(vmem_limit_bytes=40 * 1024 * 1024),
        cost_estimate=pl.CostEstimate(flops=2 * rows * width, bytes_accessed=6 * rows * width, transcendentals=0),
    )(new, inv_rms, norm_gain[None, :])


def solution(mesh):
    in_specs = (
        P("ctx", "tp"),
        P("ctx", "tp"),
        P("ctx", "tp"),
        P(None, "tp"),
        P(None, "tp"),
        P("tp"),
        P("ctx", "tp"),
        P("tp"),
    )
    out_specs = (P("ctx", "tp"), P("ctx", "tp"))
    return jax.shard_map(
        functools.partial(shards, mesh.shape["ctx"], mesh.shape["tp"]),
        mesh=mesh, in_specs=in_specs, out_specs=out_specs, check_vma=False,
    )
```

```python
import functools
import math

import jax
import jax.numpy as jnp
import numpy as np
from jax import lax
from jax.experimental import pallas as pl
from jax.experimental.pallas import tpu as pltpu
from jax.sharding import PartitionSpec as P

epsilon = 1e-06
lane = 128
sub = 8
dft_cols = 256
MESH = pl.DeviceIdType.MESH
f32 = jnp.float32
bf16 = jnp.bfloat16


def tree_sum(terms):
    while len(terms) > 1:
        terms = [a + b for a, b in zip(terms[::2], terms[1::2])] + terms[len(terms) // 2 * 2:]
    return terms[0]


def dft_tables(rows):
    freq = np.arange(rows)[:, None]
    pos = np.arange(rows)[None, :]
    angle = math.pi * (((2 * freq + 1) * pos) % (4 * rows)) / (2 * rows)
    forward = np.concatenate([np.cos(angle), -np.sin(angle)], axis=0)
    inverse = np.concatenate([np.cos(angle).T, -np.sin(angle).T], axis=0) / rows
    return np.ascontiguousarray(forward.astype(bf16)), np.ascontiguousarray(inverse.astype(bf16))


def body(
    n_ctx, n_tp, n_sub, per_dev, chunk,
    q_hbm, k_hbm, v_hbm, res_hbm, dec_hbm, skip_hbm, str_hbm, fwd_hbm, inv_hbm,
    new, inv_rms,
    q, k, v, res, dec, skip, stream, fwd, inv,
    sig, taps, conv, ends, mids, decay_pow, got, starts, states, square, row_sums,
    in_sem, gate_sem, send1, recv1, send2, recv2, send3, recv3,
):
    rows, width = q.shape
    modes = res.shape[0]
    n_lane = width // lane
    n_chunk = rows // chunk
    part = modes // n_sub
    me = lax.axis_index("ctx")
    tp = lax.axis_index("tp")

    share_width = width // n_ctx if n_sub == 1 else width

    def gate_loads(d):
        if n_sub == 1:
            first = lax.rem(me + d, n_ctx) * share_width
            cols = pl.ds(pl.multiple_of(first, share_width), share_width)
        else:
            cols = pl.ds(0, width)
        return [
            pltpu.make_async_copy(src.at[:, cols], dst.at[:, cols], gate_sem.at[i, d])
            for i, (src, dst) in enumerate(((q_hbm, q), (k_hbm, k)))
        ]

    def start_gates(d):
        for copy in gate_loads(d):
            copy.start()

    def wait_gates(d):
        for copy in gate_loads(d):
            copy.wait()

    order = [
        (dec_hbm, dec), (res_hbm, res), (fwd_hbm, fwd), (inv_hbm, inv), (skip_hbm, skip),
        (v_hbm, v), (str_hbm, stream),
    ]
    loads = [pltpu.make_async_copy(src, dst, in_sem.at[i]) for i, (src, dst) in enumerate(order)]
    loads[0].start()
    start_gates(1)

    barrier = pltpu.get_barrier_semaphore()
    for d in range(1, n_ctx):
        pl.semaphore_signal(barrier, inc=1, device_id={"ctx": lax.rem(me + d, n_ctx)}, device_id_type=MESH)
    for d in range(1, n_tp):
        pl.semaphore_signal(barrier, inc=1, device_id={"tp": lax.rem(tp + d, n_tp)}, device_id_type=MESH)

    sublane = lax.broadcasted_iota(jnp.int32, (sub, lane), 0).astype(f32)

    def lanes_of(t):
        return pl.ds(pl.multiple_of(t * lane, lane), lane)

    def spread(x, n):
        return jnp.broadcast_to(x[n:n + 1, :], (sub, lane))

    def rows_of(h, m):
        return pl.ds(pl.multiple_of(h * chunk + m * 16, 16), 16)

    def end_states(t):
        cols = lanes_of(t)
        rate = dec[:, cols]
        step = jnp.exp(rate * (-float(sub)))
        steps = [spread(step, n) for n in range(modes)]
        tails = [jnp.exp(-spread(rate, n) * (sub - 1.0 - sublane)) for n in range(modes)]
        acc = (jnp.zeros((sub, lane), f32),) * modes
        for h in range(n_chunk):

            def block(m, acc):
                at = rows_of(h, m)
                s = (q[at, cols].astype(f32) * k[at, cols].astype(f32)).astype(bf16)
                sig[at, cols] = s
                s = s.astype(f32)
                acc = tuple(a * b + s[:8] for a, b in zip(acc, steps))
                return tuple(a * b + s[8:] for a, b in zip(acc, steps))

            acc = lax.fori_loop(0, chunk // 16, block, acc, unroll=True)
            total = jnp.concatenate(
                [jnp.sum(a * w, axis=0, keepdims=True) for a, w in zip(acc, tails)], axis=0
            )
            if h < n_chunk - 1:
                mids[h, t] = total
        power = jnp.exp(rate * (-float(rows)))
        for g in range(n_sub):
            ends[t * n_sub + g] = total[g * part:(g + 1) * part]
            decay_pow[t * n_sub + g] = power[g * part:(g + 1) * part]

    def loop(first, last, step):
        def run(i, _):
            step(i)
            return 0

        lax.fori_loop(first, last, run, 0)

    if n_sub == 1:
        loop(2, n_ctx, start_gates)
        start_gates(0)
    loads[0].wait()
    mine = pl.ds(me * per_dev, per_dev)

    def copy_ends(d):
        to = lax.rem(me + d, n_ctx)
        return pltpu.make_async_remote_copy(
            src_ref=ends.at[pl.ds(to * per_dev, per_dev)], dst_ref=got.at[me],
            send_sem=send1.at[d], recv_sem=recv1.at[d], device_id={"ctx": to}, device_id_type=MESH,
        )

    if n_sub == 1:
        def share(d):
            wait_gates(d)
            for i in range(per_dev):
                end_states(lax.rem(me + d, n_ctx) * per_dev + i)

        share(1)
        for copy in loads[1:]:
            copy.start()
        pl.semaphore_wait(barrier, n_ctx - 1 + n_tp - 1)
        copy_ends(1).start()

        def share_and_send(d):
            share(d)
            copy_ends(d).start()

        loop(2, n_ctx, share_and_send)
        share(0)
    else:
        wait_gates(1)
        for copy in loads[1:]:
            copy.start()
        loop(0, n_lane, end_states)
        pl.semaphore_wait(barrier, n_ctx - 1 + n_tp - 1)
        loop(1, n_ctx, lambda d: copy_ends(d).start())

    def modal(h, coefs, steps, emit):
        def block(m, z):
            top = tree_sum(list(z))
            z = tuple(a * b for a, b in zip(z, steps))
            low = tree_sum(list(z))
            z = tuple(a * b for a, b in zip(z, steps))
            emit(rows_of(h, m), jnp.concatenate([top, low], axis=0))
            return z

        lax.fori_loop(0, chunk // 16, block, tuple(coefs), unroll=True)

    for copy in loads[1:]:
        copy.wait()

    def local_part(c):
        for i in range(dft_cols // lane):
            cols = lanes_of(c * (dft_cols // lane) + i)
            rate = dec[:, cols]
            weight = res[:, cols]
            step = jnp.exp(rate * (-float(sub)))
            steps = [spread(step, n) for n in range(modes)]
            coefs = [spread(weight, n) * jnp.exp(-spread(rate, n) * sublane) for n in range(modes)]

            def emit(at, value):
                taps[at, i * lane:(i + 1) * lane] = value.astype(bf16)

            modal(0, coefs, steps, emit)

        cols = pl.ds(pl.multiple_of(c * dft_cols, dft_cols), dft_cols)
        table = fwd[...]
        back = jnp.concatenate([inv[:chunk, :], inv[chunk:, :]], axis=1)
        g = jnp.dot(table, taps[...], preferred_element_type=f32)
        gr, gi = g[:chunk], g[chunk:]
        direct = skip[:, cols]
        for h in range(n_chunk):
            at = pl.ds(h * chunk, chunk)
            part_sig = sig[at, cols]
            u = jnp.dot(table, part_sig, preferred_element_type=f32)
            ur, ui = u[:chunk], u[chunk:]
            prod = jnp.concatenate([ur * gr - ui * gi, ur * gi + ui * gr], axis=0).astype(bf16)
            value = jnp.dot(back, prod, preferred_element_type=f32) + direct * part_sig.astype(f32)
            conv[at, cols] = stream[at, cols].astype(f32) + v[at, cols].astype(f32) * value

    n_local = width // dft_cols
    loop(0, n_local // 2, local_part)

    loop(1, n_ctx, lambda d: copy_ends(d).wait_recv())
    got[me] = ends[mine]
    power = decay_pow[mine]
    running = jnp.zeros_like(power)
    for j in range(n_ctx):
        starts[j] = running
        running = running * power + got[j]

    def copy_starts(d):
        to = lax.rem(me + d, n_ctx)
        return pltpu.make_async_remote_copy(
            src_ref=starts.at[to], dst_ref=states.at[mine],
            send_sem=send2.at[d], recv_sem=recv2.at[d], device_id={"ctx": to}, device_id_type=MESH,
        )

    loop(1, n_ctx, lambda d: copy_starts(d).start())
    states[mine] = starts[me]

    loop(n_local // 2, n_local, local_part)

    square[...] = jnp.zeros_like(square)

    def finish(t):
        cols = lanes_of(t)
        rate = dec[:, cols]
        state = jnp.concatenate([states[t * n_sub + g] for g in range(n_sub)], axis=0)
        weight = res[:, cols]
        step = jnp.exp(rate * (-float(sub)))
        steps = [spread(step, n) for n in range(modes)]
        heads = [jnp.exp(-spread(rate, n) * (sublane + 1.0)) for n in range(modes)]

        def emit(at, value):
            out = (conv[at, cols] + v[at, cols].astype(f32) * value).astype(bf16)
            new[at, cols] = out
            out = out.astype(f32)
            square[at, :] += out * out

        for h in range(n_chunk):
            now = state if h == 0 else state * jnp.exp(rate * (-float(h * chunk))) + mids[h - 1, t]
            now = now * weight
            modal(h, [spread(now, n) * w for n, w in enumerate(heads)], steps, emit)

    if n_sub == 1:
        def finish_share(d):
            frm = lax.rem(me - d + n_ctx, n_ctx)
            for i in range(per_dev):
                finish(frm * per_dev + i)

        def wait_and_finish(d):
            frm = lax.rem(me - d + n_ctx, n_ctx)
            pltpu.make_async_remote_copy(
                src_ref=starts.at[me], dst_ref=states.at[pl.ds(frm * per_dev, per_dev)],
                send_sem=send2.at[d], recv_sem=recv2.at[d], device_id={"ctx": frm}, device_id_type=MESH,
            ).wait_recv()
            finish_share(d)

        finish_share(0)
        loop(1, n_ctx, wait_and_finish)
    else:
        loop(1, n_ctx, lambda d: copy_starts(d).wait_recv())
        loop(0, n_lane, finish)

    ones = jnp.ones((sub, lane), f32)
    row_sums[tp] = lax.dot_general(
        ones, square[...], (((1,), (1,)), ((), ())),
        precision=lax.Precision.HIGHEST, preferred_element_type=f32,
    )
    third = []
    for d in range(1, n_tp):
        to = lax.rem(tp + d, n_tp)
        copy = pltpu.make_async_remote_copy(
            src_ref=row_sums.at[tp], dst_ref=row_sums.at[tp],
            send_sem=send3.at[d], recv_sem=recv3.at[d], device_id={"tp": to}, device_id_type=MESH,
        )
        copy.start()
        third.append(copy)
    loop(1, n_ctx, lambda d: copy_ends(d).wait_send())
    loop(1, n_ctx, lambda d: copy_starts(d).wait_send())
    for copy in third:
        copy.wait_recv()
    total = row_sums[0]
    for j in range(1, n_tp):
        total = total + row_sums[j]
    mean = lax.dot_general(
        total, jnp.full((sub, lane), 1.0 / sub, f32), (((0,), (0,)), ((), ())),
        precision=lax.Precision.HIGHEST, preferred_element_type=f32,
    ) / (width * n_tp)
    inv_rms[...] = lax.rsqrt(mean + epsilon)
    for copy in third:
        copy.wait_send()


def scale_body(new, inv_rms, gain, new_hbm, norm_hbm, norm, sems):
    rows, width = new.shape
    writes = [pltpu.make_async_copy(new, new_hbm, sems.at[0])]
    writes[0].start()
    piece = rows // 4
    for p in range(4):
        at = pl.ds(p * piece, piece)
        factor = inv_rms[at, :]

        def scale(t, _):
            cols = pl.ds(pl.multiple_of(t * lane, lane), lane)
            norm[at, cols] = (new[at, cols].astype(f32) * factor * gain[:, cols]).astype(bf16)
            return 0

        lax.fori_loop(0, width // lane, scale, 0, unroll=4)
        writes.append(pltpu.make_async_copy(norm.at[at], norm_hbm.at[at], sems.at[p + 1]))
        writes[-1].start()
    for write in writes:
        write.wait()


def shards(n_ctx, n_tp, queries, key_proj, values, residues, decay_rates, skip_weight, stream, norm_gain):
    rows, width = queries.shape
    modes = residues.shape[0]
    n_lane = width // lane
    n_sub = max(1, n_ctx // n_lane)
    part = modes // n_sub
    blocks = n_lane * n_sub
    per_dev = blocks // n_ctx
    chunk = rows // 2
    assert per_dev * n_ctx == blocks and part * n_sub == modes
    forward, inverse = dft_tables(chunk)
    slab = pltpu.VMEM((rows, width), bf16)
    wide = pltpu.VMEM((modes, width), f32)
    line = pltpu.VMEM((1, width), f32)
    dma = pltpu.SemaphoreType.DMA
    whole = pl.BlockSpec(memory_space=pl.ANY)
    near = pl.BlockSpec(memory_space=pltpu.VMEM)
    out = jax.ShapeDtypeStruct((rows, width), bf16)
    args = (
        queries, key_proj, values, residues, decay_rates, skip_weight[None, :], stream,
        jnp.asarray(forward), jnp.asarray(inverse),
    )
    new, inv_rms = pl.pallas_call(
        functools.partial(body, n_ctx, n_tp, n_sub, per_dev, chunk),
        out_shape=(pltpu.VMEM((rows, width), bf16), pltpu.VMEM((rows, lane), f32)),
        in_specs=[whole] * 9,
        out_specs=(near, near),
        scratch_shapes=[
            slab, slab, slab, wide, wide, line, slab,
            pltpu.VMEM((2 * chunk, chunk), bf16), pltpu.VMEM((2 * chunk, chunk), bf16),
            slab, pltpu.VMEM((chunk, dft_cols), bf16), pltpu.VMEM((rows, width), f32),
            pltpu.VMEM((blocks, part, lane), f32),
            pltpu.VMEM((rows // chunk - 1, n_lane, modes, lane), f32),
            pltpu.VMEM((blocks, part, lane), f32),
            pltpu.VMEM((n_ctx, per_dev, part, lane), f32),
            pltpu.VMEM((n_ctx, per_dev, part, lane), f32),
            pltpu.VMEM((blocks, part, lane), f32),
            pltpu.VMEM((rows, lane), f32),
            pltpu.VMEM((n_tp, sub, rows), f32),
            dma((7,)), dma((2, n_ctx)),
            dma((n_ctx,)), dma((n_ctx,)), dma((n_ctx,)), dma((n_ctx,)), dma((n_tp,)), dma((n_tp,)),
        ],
        compiler_params=pltpu.CompilerParams(
            collective_id=0, has_side_effects=True, vmem_limit_bytes=40 * 1024 * 1024
        ),
        cost_estimate=pl.CostEstimate(
            flops=6 * rows * rows * width * 2, bytes_accessed=6 * rows * width * 2, transcendentals=0
        ),
    )(*[pltpu.with_memory_space_constraint(x, pltpu.HBM) for x in args])
    return pl.pallas_call(
        scale_body,
        out_shape=(out, out),
        in_specs=[near] * 3,
        out_specs=(whole, whole),
        scratch_shapes=[slab, dma((5,))],
        compiler_params=pltpu.CompilerParams(vmem_limit_bytes=40 * 1024 * 1024),
        cost_estimate=pl.CostEstimate(flops=2 * rows * width, bytes_accessed=6 * rows * width, transcendentals=0),
    )(new, inv_rms, norm_gain[None, :])


def solution(mesh):
    in_specs = (
        P("ctx", "tp"),
        P("ctx", "tp"),
        P("ctx", "tp"),
        P(None, "tp"),
        P(None, "tp"),
        P("tp"),
        P("ctx", "tp"),
        P("tp"),
    )
    out_specs = (P("ctx", "tp"), P("ctx", "tp"))
    return jax.shard_map(
        functools.partial(shards, mesh.shape["ctx"], mesh.shape["tp"]),
        mesh=mesh, in_specs=in_specs, out_specs=out_specs, check_vma=False,
    )
```

```python
import functools
import math

import jax
import jax.numpy as jnp
import numpy as np
from jax import lax
from jax.experimental import pallas as pl
from jax.experimental.pallas import tpu as pltpu
from jax.sharding import PartitionSpec as P

epsilon = 1e-06
lane = 128
sub = 8
dft_cols = 256
MESH = pl.DeviceIdType.MESH
f32 = jnp.float32
bf16 = jnp.bfloat16


def tree_sum(terms):
    while len(terms) > 1:
        terms = [a + b for a, b in zip(terms[::2], terms[1::2])] + terms[len(terms) // 2 * 2:]
    return terms[0]


def dft_tables(rows):
    freq = np.arange(rows)[:, None]
    pos = np.arange(rows)[None, :]
    angle = math.pi * (((2 * freq + 1) * pos) % (4 * rows)) / (2 * rows)
    forward = np.concatenate([np.cos(angle), -np.sin(angle)], axis=0)
    inverse = np.concatenate([np.cos(angle).T, -np.sin(angle).T], axis=0) / rows
    return np.ascontiguousarray(forward.astype(bf16)), np.ascontiguousarray(inverse.astype(bf16))


def body(
    n_ctx, n_tp, piece, chunk,
    q_hbm, k_hbm, v_hbm, res_hbm, dec_hbm, skip_hbm, str_hbm, fwd_hbm, inv_hbm,
    new, inv_rms,
    q, k, v, res, dec, skip, stream, fwd, inv,
    sig, taps, conv, ends, mids, decay_pow, got, chain_in, chain_out, starts, states, square, row_sums,
    in_sem, gate_sem, send1, recv1, send2, recv2, send3, recv3, send4, recv4,
):
    rows, width = q.shape
    modes = res.shape[0]
    n_lane = width // lane
    n_chunk = rows // chunk
    me = lax.axis_index("ctx")
    tp = lax.axis_index("tp")
    odd = lax.rem(me, 2)
    pair = me // 2
    n_pair = n_ctx // 2
    mate = me + 1 - 2 * odd
    half = n_lane // 2
    n_piece = half // piece
    own_first = odd * half
    mate_first = half - own_first

    width_piece = piece * lane

    def tile_of(g):
        return lax.rem(mate_first + g * piece, n_lane)

    def gate_loads(g):
        cols = pl.ds(pl.multiple_of(tile_of(g) * lane, width_piece), width_piece)
        return [
            pltpu.make_async_copy(src.at[:, cols], dst.at[:, cols], gate_sem.at[i, g])
            for i, (src, dst) in enumerate(((q_hbm, q), (k_hbm, k)))
        ]

    def start_gates(g):
        for copy in gate_loads(g):
            copy.start()

    def wait_gates(g):
        for copy in gate_loads(g):
            copy.wait()

    order = [
        (dec_hbm, dec), (res_hbm, res), (fwd_hbm, fwd), (inv_hbm, inv), (skip_hbm, skip),
        (v_hbm, v), (str_hbm, stream),
    ]
    loads = [pltpu.make_async_copy(src, dst, in_sem.at[i]) for i, (src, dst) in enumerate(order)]
    loads[0].start()
    start_gates(0)

    barrier = pltpu.get_barrier_semaphore()
    pl.semaphore_signal(barrier, inc=1, device_id={"ctx": mate}, device_id_type=MESH)

    @pl.when(pair > 0)
    def _():
        pl.semaphore_signal(barrier, inc=1, device_id={"ctx": lax.rem(me + n_ctx - 2, n_ctx)}, device_id_type=MESH)

    for d in range(1, n_tp):
        pl.semaphore_signal(barrier, inc=1, device_id={"tp": lax.rem(tp + d, n_tp)}, device_id_type=MESH)

    sublane = lax.broadcasted_iota(jnp.int32, (sub, lane), 0).astype(f32)

    def lanes_of(t):
        return pl.ds(pl.multiple_of(t * lane, lane), lane)

    def spread(x, n):
        return jnp.broadcast_to(x[n:n + 1, :], (sub, lane))

    def rows_of(h, m):
        return pl.ds(pl.multiple_of(h * chunk + m * 16, 16), 16)

    def end_states(t):
        cols = lanes_of(t)
        rate = dec[:, cols]
        step = jnp.exp(rate * (-float(sub)))
        steps = [spread(step, n) for n in range(modes)]
        tails = [jnp.exp(-spread(rate, n) * (sub - 1.0 - sublane)) for n in range(modes)]
        acc = (jnp.zeros((sub, lane), f32),) * modes
        for h in range(n_chunk):

            def block(m, acc):
                at = rows_of(h, m)
                s = (q[at, cols].astype(f32) * k[at, cols].astype(f32)).astype(bf16)
                sig[at, cols] = s
                s = s.astype(f32)
                acc = tuple(a * b + s[:8] for a, b in zip(acc, steps))
                return tuple(a * b + s[8:] for a, b in zip(acc, steps))

            acc = lax.fori_loop(0, chunk // 16, block, acc, unroll=True)
            total = jnp.concatenate(
                [jnp.sum(a * w, axis=0, keepdims=True) for a, w in zip(acc, tails)], axis=0
            )
            if h < n_chunk - 1:
                mids[h, t] = total
        power = jnp.exp(rate * (-float(rows)))
        ends[t] = total
        decay_pow[t] = power

    def loop(first, last, step):
        def run(i, _):
            step(i)
            return 0

        lax.fori_loop(first, last, run, 0)

    loop(1, 2 * n_piece, start_gates)
    loads[0].wait()

    def piece_of(first, g):
        return pl.ds(first + g * piece, piece)

    def copy_ends(g):
        return pltpu.make_async_remote_copy(
            src_ref=ends.at[piece_of(mate_first, g)], dst_ref=got.at[piece_of(0, g)],
            send_sem=send1.at[g], recv_sem=recv1.at[g], device_id={"ctx": mate}, device_id_type=MESH,
        )

    def copy_chain(g):
        return pltpu.make_async_remote_copy(
            src_ref=chain_out.at[piece_of(0, g)], dst_ref=chain_in.at[piece_of(0, g)],
            send_sem=send4.at[g], recv_sem=recv4.at[g],
            device_id={"ctx": lax.rem(me + 2, n_ctx)}, device_id_type=MESH,
        )

    def copy_starts(g):
        return pltpu.make_async_remote_copy(
            src_ref=starts.at[piece_of(0, g)], dst_ref=states.at[piece_of(own_first, g)],
            send_sem=send2.at[g], recv_sem=recv2.at[g], device_id={"ctx": mate}, device_id_type=MESH,
        )

    def piece_ends(g):
        wait_gates(g)
        for i in range(piece):
            end_states(tile_of(g) + i)

    piece_ends(0)
    for copy in loads[1:]:
        copy.start()
    pl.semaphore_wait(barrier, n_tp + jnp.minimum(n_pair - 1 - pair, 1))
    copy_ends(0).start()

    def ends_and_send(g):
        piece_ends(g)
        copy_ends(g).start()

    loop(1, n_piece, ends_and_send)
    loop(n_piece, 2 * n_piece, piece_ends)

    def modal(h, coefs, steps, emit):
        def block(m, z):
            top = tree_sum(list(z))
            z = tuple(a * b for a, b in zip(z, steps))
            low = tree_sum(list(z))
            z = tuple(a * b for a, b in zip(z, steps))
            emit(rows_of(h, m), jnp.concatenate([top, low], axis=0))
            return z

        lax.fori_loop(0, chunk // 16, block, tuple(coefs), unroll=True)

    for copy in loads[1:]:
        copy.wait()

    def local_part(c):
        for i in range(dft_cols // lane):
            cols = lanes_of(c * (dft_cols // lane) + i)
            rate = dec[:, cols]
            weight = res[:, cols]
            step = jnp.exp(rate * (-float(sub)))
            steps = [spread(step, n) for n in range(modes)]
            coefs = [spread(weight, n) * jnp.exp(-spread(rate, n) * sublane) for n in range(modes)]

            def emit(at, value):
                taps[at, i * lane:(i + 1) * lane] = value.astype(bf16)

            modal(0, coefs, steps, emit)

        cols = pl.ds(pl.multiple_of(c * dft_cols, dft_cols), dft_cols)
        table = fwd[...]
        back = jnp.concatenate([inv[:chunk, :], inv[chunk:, :]], axis=1)
        g = jnp.dot(table, taps[...], preferred_element_type=f32)
        gr, gi = g[:chunk], g[chunk:]
        direct = skip[:, cols]
        for h in range(n_chunk):
            at = pl.ds(h * chunk, chunk)
            part_sig = sig[at, cols]
            u = jnp.dot(table, part_sig, preferred_element_type=f32)
            ur, ui = u[:chunk], u[chunk:]
            prod = jnp.concatenate([ur * gr - ui * gi, ur * gi + ui * gr], axis=0).astype(bf16)
            value = jnp.dot(back, prod, preferred_element_type=f32) + direct * part_sig.astype(f32)
            conv[at, cols] = stream[at, cols].astype(f32) + v[at, cols].astype(f32) * value

    n_local = width // dft_cols
    before = jnp.minimum(2 * pair, n_local)
    loop(0, before, local_part)

    @pl.when(pair == 0)
    def _():
        chain_in[...] = jnp.zeros_like(chain_in)

    def pass_on(g):
        copy_ends(g).wait_recv()

        @pl.when(pair > 0)
        def _():
            copy_chain(g).wait_recv()

        here = piece_of(0, g)
        own = piece_of(own_first, g)
        power = decay_pow[own]
        is_odd = odd == 1
        first_end = jnp.where(is_odd, got[here], ends[own])
        last_end = jnp.where(is_odd, ends[own], got[here])
        even_start = chain_in[here]
        odd_start = power * even_start + first_end
        chain_out[here] = power * odd_start + last_end

        @pl.when(pair < n_pair - 1)
        def _():
            copy_chain(g).start()

        states[own] = jnp.where(is_odd, odd_start, even_start)
        starts[here] = jnp.where(is_odd, even_start, odd_start)
        copy_starts(g).start()

    loop(0, n_piece, pass_on)
    loop(before, n_local, local_part)

    square[...] = jnp.zeros_like(square)

    def finish(t):
        cols = lanes_of(t)
        rate = dec[:, cols]
        state = states[t]
        weight = res[:, cols]
        step = jnp.exp(rate * (-float(sub)))
        steps = [spread(step, n) for n in range(modes)]
        heads = [jnp.exp(-spread(rate, n) * (sublane + 1.0)) for n in range(modes)]

        def emit(at, value):
            out = (conv[at, cols] + v[at, cols].astype(f32) * value).astype(bf16)
            new[at, cols] = out
            out = out.astype(f32)
            square[at, :] += out * out

        for h in range(n_chunk):
            now = state if h == 0 else state * jnp.exp(rate * (-float(h * chunk))) + mids[h - 1, t]
            now = now * weight
            modal(h, [spread(now, n) * w for n, w in enumerate(heads)], steps, emit)

    def finish_own(g):
        for i in range(piece):
            finish(own_first + g * piece + i)

    def finish_mate(g):
        pltpu.make_async_remote_copy(
            src_ref=starts.at[piece_of(0, g)], dst_ref=states.at[piece_of(mate_first, g)],
            send_sem=send2.at[g], recv_sem=recv2.at[g], device_id={"ctx": mate}, device_id_type=MESH,
        ).wait_recv()
        for i in range(piece):
            finish(mate_first + g * piece + i)

    loop(0, n_piece, finish_own)
    loop(0, n_piece, finish_mate)

    ones = jnp.ones((sub, lane), f32)
    row_sums[tp] = lax.dot_general(
        ones, square[...], (((1,), (1,)), ((), ())),
        precision=lax.Precision.HIGHEST, preferred_element_type=f32,
    )
    third = []
    for d in range(1, n_tp):
        to = lax.rem(tp + d, n_tp)
        copy = pltpu.make_async_remote_copy(
            src_ref=row_sums.at[tp], dst_ref=row_sums.at[tp],
            send_sem=send3.at[d], recv_sem=recv3.at[d], device_id={"tp": to}, device_id_type=MESH,
        )
        copy.start()
        third.append(copy)
    loop(0, n_piece, lambda g: copy_ends(g).wait_send())
    loop(0, n_piece, lambda g: copy_starts(g).wait_send())

    @pl.when(pair < n_pair - 1)
    def _():
        loop(0, n_piece, lambda g: copy_chain(g).wait_send())

    for copy in third:
        copy.wait_recv()
    total = row_sums[0]
    for j in range(1, n_tp):
        total = total + row_sums[j]
    mean = lax.dot_general(
        total, jnp.full((sub, lane), 1.0 / sub, f32), (((0,), (0,)), ((), ())),
        precision=lax.Precision.HIGHEST, preferred_element_type=f32,
    ) / (width * n_tp)
    inv_rms[...] = lax.rsqrt(mean + epsilon)
    for copy in third:
        copy.wait_send()


def scale_body(new, inv_rms, gain, new_hbm, norm_hbm, norm, sems):
    rows, width = new.shape
    writes = [pltpu.make_async_copy(new, new_hbm, sems.at[0])]
    writes[0].start()
    piece = rows // 4
    for p in range(4):
        at = pl.ds(p * piece, piece)
        factor = inv_rms[at, :]

        def scale(t, _):
            cols = pl.ds(pl.multiple_of(t * lane, lane), lane)
            norm[at, cols] = (new[at, cols].astype(f32) * factor * gain[:, cols]).astype(bf16)
            return 0

        lax.fori_loop(0, width // lane, scale, 0, unroll=4)
        writes.append(pltpu.make_async_copy(norm.at[at], norm_hbm.at[at], sems.at[p + 1]))
        writes[-1].start()
    for write in writes:
        write.wait()


def shards(n_ctx, n_tp, queries, key_proj, values, residues, decay_rates, skip_weight, stream, norm_gain):
    rows, width = queries.shape
    modes = residues.shape[0]
    n_lane = width // lane
    half = n_lane // 2
    piece = 2
    n_piece = half // piece
    chunk = rows // 2
    assert n_ctx % 2 == 0 and n_piece * piece * 2 == n_lane
    forward, inverse = dft_tables(chunk)
    slab = pltpu.VMEM((rows, width), bf16)
    wide = pltpu.VMEM((modes, width), f32)
    line = pltpu.VMEM((1, width), f32)
    dma = pltpu.SemaphoreType.DMA
    whole = pl.BlockSpec(memory_space=pl.ANY)
    near = pl.BlockSpec(memory_space=pltpu.VMEM)
    out = jax.ShapeDtypeStruct((rows, width), bf16)
    args = (
        queries, key_proj, values, residues, decay_rates, skip_weight[None, :], stream,
        jnp.asarray(forward), jnp.asarray(inverse),
    )
    new, inv_rms = pl.pallas_call(
        functools.partial(body, n_ctx, n_tp, piece, chunk),
        out_shape=(pltpu.VMEM((rows, width), bf16), pltpu.VMEM((rows, lane), f32)),
        in_specs=[whole] * 9,
        out_specs=(near, near),
        scratch_shapes=[
            slab, slab, slab, wide, wide, line, slab,
            pltpu.VMEM((2 * chunk, chunk), bf16), pltpu.VMEM((2 * chunk, chunk), bf16),
            slab, pltpu.VMEM((chunk, dft_cols), bf16), pltpu.VMEM((rows, width), f32),
            pltpu.VMEM((n_lane, modes, lane), f32),
            pltpu.VMEM((rows // chunk - 1, n_lane, modes, lane), f32),
            pltpu.VMEM((n_lane, modes, lane), f32),
            pltpu.VMEM((half, modes, lane), f32),
            pltpu.VMEM((half, modes, lane), f32),
            pltpu.VMEM((half, modes, lane), f32),
            pltpu.VMEM((half, modes, lane), f32),
            pltpu.VMEM((n_lane, modes, lane), f32),
            pltpu.VMEM((rows, lane), f32),
            pltpu.VMEM((n_tp, sub, rows), f32),
            dma((7,)), dma((2, 2 * n_piece)),
            dma((n_piece,)), dma((n_piece,)), dma((n_piece,)), dma((n_piece,)),
            dma((n_tp,)), dma((n_tp,)), dma((n_piece,)), dma((n_piece,)),
        ],
        compiler_params=pltpu.CompilerParams(
            collective_id=0, has_side_effects=True, vmem_limit_bytes=40 * 1024 * 1024
        ),
        cost_estimate=pl.CostEstimate(
            flops=6 * rows * rows * width * 2, bytes_accessed=6 * rows * width * 2, transcendentals=0
        ),
    )(*[pltpu.with_memory_space_constraint(x, pltpu.HBM) for x in args])
    return pl.pallas_call(
        scale_body,
        out_shape=(out, out),
        in_specs=[near] * 3,
        out_specs=(whole, whole),
        scratch_shapes=[slab, dma((5,))],
        compiler_params=pltpu.CompilerParams(vmem_limit_bytes=40 * 1024 * 1024),
        cost_estimate=pl.CostEstimate(flops=2 * rows * width, bytes_accessed=6 * rows * width, transcendentals=0),
    )(new, inv_rms, norm_gain[None, :])


def solution(mesh):
    in_specs = (
        P("ctx", "tp"),
        P("ctx", "tp"),
        P("ctx", "tp"),
        P(None, "tp"),
        P(None, "tp"),
        P("tp"),
        P("ctx", "tp"),
        P("tp"),
    )
    out_specs = (P("ctx", "tp"), P("ctx", "tp"))
    return jax.shard_map(
        functools.partial(shards, mesh.shape["ctx"], mesh.shape["tp"]),
        mesh=mesh, in_specs=in_specs, out_specs=out_specs, check_vma=False,
    )
```

```python
import functools
import math

import jax
import jax.numpy as jnp
import numpy as np
from jax import lax
from jax.experimental import pallas as pl
from jax.experimental.pallas import tpu as pltpu
from jax.sharding import PartitionSpec as P

epsilon = 1e-06
lane = 128
sub = 8
dft_cols = 256
MESH = pl.DeviceIdType.MESH
f32 = jnp.float32
bf16 = jnp.bfloat16


def tree_sum(terms):
    while len(terms) > 1:
        terms = [a + b for a, b in zip(terms[::2], terms[1::2])] + terms[len(terms) // 2 * 2:]
    return terms[0]


def dft_tables(rows):
    freq = np.arange(rows)[:, None]
    pos = np.arange(rows)[None, :]
    angle = math.pi * (((2 * freq + 1) * pos) % (4 * rows)) / (2 * rows)
    forward = np.concatenate([np.cos(angle), -np.sin(angle)], axis=0)
    inverse = np.concatenate([np.cos(angle).T, -np.sin(angle).T], axis=0) / rows
    return np.ascontiguousarray(forward.astype(bf16)), np.ascontiguousarray(inverse.astype(bf16))


def body(
    n_ctx, n_tp, piece, chunk,
    q_hbm, k_hbm, v_hbm, res_hbm, dec_hbm, skip_hbm, str_hbm, fwd_hbm, inv_hbm,
    new, inv_rms,
    q, k, v, res, dec, skip, stream, fwd, inv,
    sig, taps, conv, ends, mids, decay_pow, got, chain_in, chain_out, starts, states, square, row_sums,
    in_sem, gate_sem, send1, recv1, send2, recv2, send3, recv3, send4, recv4,
):
    rows, width = q.shape
    modes = res.shape[0]
    n_lane = width // lane
    n_chunk = rows // chunk
    me = lax.axis_index("ctx")
    tp = lax.axis_index("tp")
    odd = lax.rem(me, 2)
    pair = me // 2
    n_pair = n_ctx // 2
    mate = me + 1 - 2 * odd
    half = n_lane // 2
    n_piece = half // piece
    own_first = odd * half
    mate_first = half - own_first

    width_piece = piece * lane

    def tile_of(g):
        return lax.rem(mate_first + g * piece, n_lane)

    def gate_loads(g):
        cols = pl.ds(pl.multiple_of(tile_of(g) * lane, width_piece), width_piece)
        return [
            pltpu.make_async_copy(src.at[:, cols], dst.at[:, cols], gate_sem.at[i, g])
            for i, (src, dst) in enumerate(((q_hbm, q), (k_hbm, k)))
        ]

    def start_gates(g):
        for copy in gate_loads(g):
            copy.start()

    def wait_gates(g):
        for copy in gate_loads(g):
            copy.wait()

    order = [
        (dec_hbm, dec), (res_hbm, res), (fwd_hbm, fwd), (inv_hbm, inv), (skip_hbm, skip),
        (v_hbm, v), (str_hbm, stream),
    ]
    loads = [pltpu.make_async_copy(src, dst, in_sem.at[i]) for i, (src, dst) in enumerate(order)]
    loads[0].start()
    start_gates(0)

    barrier = pltpu.get_barrier_semaphore()
    pl.semaphore_signal(barrier, inc=1, device_id={"ctx": mate}, device_id_type=MESH)

    @pl.when(pair > 0)
    def _():
        pl.semaphore_signal(barrier, inc=1, device_id={"ctx": lax.rem(me + n_ctx - 2, n_ctx)}, device_id_type=MESH)

    for d in range(1, n_tp):
        pl.semaphore_signal(barrier, inc=1, device_id={"tp": lax.rem(tp + d, n_tp)}, device_id_type=MESH)

    sublane = lax.broadcasted_iota(jnp.int32, (sub, lane), 0).astype(f32)

    def lanes_of(t):
        return pl.ds(pl.multiple_of(t * lane, lane), lane)

    def spread(x, n):
        return jnp.broadcast_to(x[n:n + 1, :], (sub, lane))

    def rows_of(h, m):
        return pl.ds(pl.multiple_of(h * chunk + m * 16, 16), 16)

    def end_states(t):
        cols = lanes_of(t)
        rate = dec[:, cols]
        step = jnp.exp(rate * (-float(sub)))
        steps = [spread(step, n) for n in range(modes)]
        tails = [jnp.exp(-spread(rate, n) * (sub - 1.0 - sublane)) for n in range(modes)]
        acc = (jnp.zeros((sub, lane), f32),) * modes
        for h in range(n_chunk):

            def block(m, acc):
                at = rows_of(h, m)
                s = (q[at, cols].astype(f32) * k[at, cols].astype(f32)).astype(bf16)
                sig[at, cols] = s
                s = s.astype(f32)
                acc = tuple(a * b + s[:8] for a, b in zip(acc, steps))
                return tuple(a * b + s[8:] for a, b in zip(acc, steps))

            acc = lax.fori_loop(0, chunk // 16, block, acc, unroll=True)
            total = jnp.concatenate(
                [jnp.sum(a * w, axis=0, keepdims=True) for a, w in zip(acc, tails)], axis=0
            )
            if h < n_chunk - 1:
                mids[h, t] = total
        power = jnp.exp(rate * (-float(rows)))
        ends[t] = total
        decay_pow[t] = power

    def loop(first, last, step):
        def run(i, _):
            step(i)
            return 0

        lax.fori_loop(first, last, run, 0)

    loop(1, 2 * n_piece, start_gates)
    loads[0].wait()

    def piece_of(first, g):
        return pl.ds(first + g * piece, piece)

    def copy_ends(g):
        return pltpu.make_async_remote_copy(
            src_ref=ends.at[piece_of(mate_first, g)], dst_ref=got.at[piece_of(0, g)],
            send_sem=send1.at[g], recv_sem=recv1.at[g], device_id={"ctx": mate}, device_id_type=MESH,
        )

    def copy_chain(g):
        return pltpu.make_async_remote_copy(
            src_ref=chain_out.at[piece_of(0, g)], dst_ref=chain_in.at[piece_of(0, g)],
            send_sem=send4.at[g], recv_sem=recv4.at[g],
            device_id={"ctx": lax.rem(me + 2, n_ctx)}, device_id_type=MESH,
        )

    def copy_starts(g):
        return pltpu.make_async_remote_copy(
            src_ref=starts.at[piece_of(0, g)], dst_ref=states.at[piece_of(own_first, g)],
            send_sem=send2.at[g], recv_sem=recv2.at[g], device_id={"ctx": mate}, device_id_type=MESH,
        )

    def piece_ends(g):
        wait_gates(g)
        for i in range(piece):
            end_states(tile_of(g) + i)

    piece_ends(0)
    for copy in loads[1:]:
        copy.start()
    pl.semaphore_wait(barrier, n_tp + jnp.minimum(n_pair - 1 - pair, 1))
    copy_ends(0).start()

    def ends_and_send(g):
        piece_ends(g)
        copy_ends(g).start()

    loop(1, n_piece, ends_and_send)
    loop(n_piece, 2 * n_piece, piece_ends)

    def modal(h, coefs, steps, emit):
        def block(m, z):
            top = tree_sum(list(z))
            z = tuple(a * b for a, b in zip(z, steps))
            low = tree_sum(list(z))
            z = tuple(a * b for a, b in zip(z, steps))
            emit(rows_of(h, m), jnp.concatenate([top, low], axis=0))
            return z

        lax.fori_loop(0, chunk // 16, block, tuple(coefs), unroll=True)

    for copy in loads[1:]:
        copy.wait()

    def local_part(c):
        for i in range(dft_cols // lane):
            cols = lanes_of(c * (dft_cols // lane) + i)
            rate = dec[:, cols]
            weight = res[:, cols]
            step = jnp.exp(rate * (-float(sub)))
            steps = [spread(step, n) for n in range(modes)]
            coefs = [spread(weight, n) * jnp.exp(-spread(rate, n) * sublane) for n in range(modes)]

            def emit(at, value):
                taps[at, i * lane:(i + 1) * lane] = value.astype(bf16)

            modal(0, coefs, steps, emit)

        cols = pl.ds(pl.multiple_of(c * dft_cols, dft_cols), dft_cols)
        table = fwd[...]
        back = jnp.concatenate([inv[:chunk, :], inv[chunk:, :]], axis=1)
        g = jnp.dot(table, taps[...], preferred_element_type=f32)
        gr, gi = g[:chunk], g[chunk:]
        direct = skip[:, cols]
        for h in range(n_chunk):
            at = pl.ds(h * chunk, chunk)
            part_sig = sig[at, cols]
            u = jnp.dot(table, part_sig, preferred_element_type=f32)
            ur, ui = u[:chunk], u[chunk:]
            prod = jnp.concatenate([ur * gr - ui * gi, ur * gi + ui * gr], axis=0).astype(bf16)
            value = jnp.dot(back, prod, preferred_element_type=f32) + direct * part_sig.astype(f32)
            conv[at, cols] = stream[at, cols].astype(f32) + v[at, cols].astype(f32) * value

    n_local = width // dft_cols
    before = jnp.minimum(jnp.where(pair < n_pair - 1, pair, 2 * pair), n_local)
    loop(0, before, local_part)

    @pl.when(pair == 0)
    def _():
        chain_in[...] = jnp.zeros_like(chain_in)

    def pass_on(g):
        copy_ends(g).wait_recv()

        @pl.when(pair > 0)
        def _():
            copy_chain(g).wait_recv()

        here = piece_of(0, g)
        own = piece_of(own_first, g)
        power = decay_pow[own]
        is_odd = odd == 1
        first_end = jnp.where(is_odd, got[here], ends[own])
        last_end = jnp.where(is_odd, ends[own], got[here])
        even_start = chain_in[here]
        odd_start = power * even_start + first_end
        chain_out[here] = power * odd_start + last_end

        @pl.when(pair < n_pair - 1)
        def _():
            copy_chain(g).start()

        states[own] = jnp.where(is_odd, odd_start, even_start)
        starts[here] = jnp.where(is_odd, even_start, odd_start)
        copy_starts(g).start()

    loop(0, n_piece, pass_on)
    loop(before, n_local, local_part)

    square[...] = jnp.zeros_like(square)

    def finish(t):
        cols = lanes_of(t)
        rate = dec[:, cols]
        state = states[t]
        weight = res[:, cols]
        step = jnp.exp(rate * (-float(sub)))
        steps = [spread(step, n) for n in range(modes)]
        heads = [jnp.exp(-spread(rate, n) * (sublane + 1.0)) for n in range(modes)]

        def emit(at, value):
            out = (conv[at, cols] + v[at, cols].astype(f32) * value).astype(bf16)
            new[at, cols] = out
            out = out.astype(f32)
            square[at, :] += out * out

        for h in range(n_chunk):
            now = state if h == 0 else state * jnp.exp(rate * (-float(h * chunk))) + mids[h - 1, t]
            now = now * weight
            modal(h, [spread(now, n) * w for n, w in enumerate(heads)], steps, emit)

    def finish_own(g):
        for i in range(piece):
            finish(own_first + g * piece + i)

    def finish_mate(g):
        pltpu.make_async_remote_copy(
            src_ref=starts.at[piece_of(0, g)], dst_ref=states.at[piece_of(mate_first, g)],
            send_sem=send2.at[g], recv_sem=recv2.at[g], device_id={"ctx": mate}, device_id_type=MESH,
        ).wait_recv()
        for i in range(piece):
            finish(mate_first + g * piece + i)

    loop(0, n_piece, finish_own)
    loop(0, n_piece, finish_mate)

    ones = jnp.ones((sub, lane), f32)
    row_sums[tp] = lax.dot_general(
        ones, square[...], (((1,), (1,)), ((), ())),
        precision=lax.Precision.HIGHEST, preferred_element_type=f32,
    )
    third = []
    for d in range(1, n_tp):
        to = lax.rem(tp + d, n_tp)
        copy = pltpu.make_async_remote_copy(
            src_ref=row_sums.at[tp], dst_ref=row_sums.at[tp],
            send_sem=send3.at[d], recv_sem=recv3.at[d], device_id={"tp": to}, device_id_type=MESH,
        )
        copy.start()
        third.append(copy)
    loop(0, n_piece, lambda g: copy_ends(g).wait_send())
    loop(0, n_piece, lambda g: copy_starts(g).wait_send())

    @pl.when(pair < n_pair - 1)
    def _():
        loop(0, n_piece, lambda g: copy_chain(g).wait_send())

    for copy in third:
        copy.wait_recv()
    total = row_sums[0]
    for j in range(1, n_tp):
        total = total + row_sums[j]
    mean = lax.dot_general(
        total, jnp.full((sub, lane), 1.0 / sub, f32), (((0,), (0,)), ((), ())),
        precision=lax.Precision.HIGHEST, preferred_element_type=f32,
    ) / (width * n_tp)
    inv_rms[...] = lax.rsqrt(mean + epsilon)
    for copy in third:
        copy.wait_send()


def scale_body(new, inv_rms, gain, new_hbm, norm_hbm, norm, sems):
    rows, width = new.shape
    writes = [pltpu.make_async_copy(new, new_hbm, sems.at[0])]
    writes[0].start()
    piece = rows // 4
    for p in range(4):
        at = pl.ds(p * piece, piece)
        factor = inv_rms[at, :]

        def scale(t, _):
            cols = pl.ds(pl.multiple_of(t * lane, lane), lane)
            norm[at, cols] = (new[at, cols].astype(f32) * factor * gain[:, cols]).astype(bf16)
            return 0

        lax.fori_loop(0, width // lane, scale, 0, unroll=4)
        writes.append(pltpu.make_async_copy(norm.at[at], norm_hbm.at[at], sems.at[p + 1]))
        writes[-1].start()
    for write in writes:
        write.wait()


def shards(n_ctx, n_tp, queries, key_proj, values, residues, decay_rates, skip_weight, stream, norm_gain):
    rows, width = queries.shape
    modes = residues.shape[0]
    n_lane = width // lane
    half = n_lane // 2
    piece = 2
    n_piece = half // piece
    chunk = rows // 2
    assert n_ctx % 2 == 0 and n_piece * piece * 2 == n_lane
    forward, inverse = dft_tables(chunk)
    slab = pltpu.VMEM((rows, width), bf16)
    wide = pltpu.VMEM((modes, width), f32)
    line = pltpu.VMEM((1, width), f32)
    dma = pltpu.SemaphoreType.DMA
    whole = pl.BlockSpec(memory_space=pl.ANY)
    near = pl.BlockSpec(memory_space=pltpu.VMEM)
    out = jax.ShapeDtypeStruct((rows, width), bf16)
    args = (
        queries, key_proj, values, residues, decay_rates, skip_weight[None, :], stream,
        jnp.asarray(forward), jnp.asarray(inverse),
    )
    new, inv_rms = pl.pallas_call(
        functools.partial(body, n_ctx, n_tp, piece, chunk),
        out_shape=(pltpu.VMEM((rows, width), bf16), pltpu.VMEM((rows, lane), f32)),
        in_specs=[whole] * 9,
        out_specs=(near, near),
        scratch_shapes=[
            slab, slab, slab, wide, wide, line, slab,
            pltpu.VMEM((2 * chunk, chunk), bf16), pltpu.VMEM((2 * chunk, chunk), bf16),
            slab, pltpu.VMEM((chunk, dft_cols), bf16), pltpu.VMEM((rows, width), f32),
            pltpu.VMEM((n_lane, modes, lane), f32),
            pltpu.VMEM((rows // chunk - 1, n_lane, modes, lane), f32),
            pltpu.VMEM((n_lane, modes, lane), f32),
            pltpu.VMEM((half, modes, lane), f32),
            pltpu.VMEM((half, modes, lane), f32),
            pltpu.VMEM((half, modes, lane), f32),
            pltpu.VMEM((half, modes, lane), f32),
            pltpu.VMEM((n_lane, modes, lane), f32),
            pltpu.VMEM((rows, lane), f32),
            pltpu.VMEM((n_tp, sub, rows), f32),
            dma((7,)), dma((2, 2 * n_piece)),
            dma((n_piece,)), dma((n_piece,)), dma((n_piece,)), dma((n_piece,)),
            dma((n_tp,)), dma((n_tp,)), dma((n_piece,)), dma((n_piece,)),
        ],
        compiler_params=pltpu.CompilerParams(
            collective_id=0, has_side_effects=True, vmem_limit_bytes=40 * 1024 * 1024
        ),
        cost_estimate=pl.CostEstimate(
            flops=6 * rows * rows * width * 2, bytes_accessed=6 * rows * width * 2, transcendentals=0
        ),
    )(*[pltpu.with_memory_space_constraint(x, pltpu.HBM) for x in args])
    return pl.pallas_call(
        scale_body,
        out_shape=(out, out),
        in_specs=[near] * 3,
        out_specs=(whole, whole),
        scratch_shapes=[slab, dma((5,))],
        compiler_params=pltpu.CompilerParams(vmem_limit_bytes=40 * 1024 * 1024),
        cost_estimate=pl.CostEstimate(flops=2 * rows * width, bytes_accessed=6 * rows * width, transcendentals=0),
    )(new, inv_rms, norm_gain[None, :])


def solution(mesh):
    in_specs = (
        P("ctx", "tp"),
        P("ctx", "tp"),
        P("ctx", "tp"),
        P(None, "tp"),
        P(None, "tp"),
        P("tp"),
        P("ctx", "tp"),
        P("tp"),
    )
    out_specs = (P("ctx", "tp"), P("ctx", "tp"))
    return jax.shard_map(
        functools.partial(shards, mesh.shape["ctx"], mesh.shape["tp"]),
        mesh=mesh, in_specs=in_specs, out_specs=out_specs, check_vma=False,
    )
```
